128 devices in a mesh: blk: 32 (over x, y, z_lo), rep: 4 (over z_hi, core).
Axes of the slice: x: 4, y: 4, z: 4 (z_hi: 2, z_lo: 2; z = z_hi * 2 + z_lo), core: 2. Of those that a mesh axis runs over, the one named last changes fastest.
Arguments:
- tile_values: bfloat16 [32, 4, 32, 1, 256, 256], P('blk', 'rep'), may hold values from -0.1875 to 0.1875
- tile_rows: int32 [32, 4, 32, 1], P('blk', 'rep'), may hold values from 0 to 1, as said below
- tile_cols: int32 [32, 4, 32, 1], P('blk', 'rep'), may hold values from 0 to 1
- tile_counts: int32 [32, 4, 32], P('blk', 'rep'), may hold values from 0 to 1, as said below
- grad_out: bfloat16 [16384, 512], P('blk'), may hold values from -6 to 6
- features: bfloat16 [16384, 512], P(('blk', 'rep')), may hold values from -0.125 to 0.125
- weight: bfloat16 [512, 512], replicated, may hold values from -0.25 to 0.25
Outputs:
- grad_features: float32 [16384, 512], P(('blk', 'rep'))
- grad_weight: float32 [512, 512], replicated
The draws below stay inside these ranges and needn't reach their ends.
Inputs may be any that keep to these rules, and one draw needn't show every extreme that they name: `tile_counts`: every device has some column block with all 1 slots used. `tile_rows`: for each row block and column block, the slots of all devices of that row block lie at distinct tile positions.
All inputs are finite; a program needn't handle non-finite values.
Results may differ from the reference program's by a relative error of at most 0.0029.
Values may be sent and summed in bfloat16 or wider, within the bound.
A program may use at most 128 MiB of HBM per device.

```python
import jax
import jax.numpy as jnp
from jax import lax

F = 512
DIN = 512
TILE = 256
BLK_NODES = 512
SLOTS = 1
NBLK = 32
REPS = 4
RT = 2
NODES = 16384
N_BLK = 32


def tile_positions(key):
    cells = RT * RT
    scores = jax.random.randint(key, (NBLK, NBLK, cells), 0, 1 << 20) * cells + jnp.arange(cells, dtype=jnp.int32)[None, None, :]
    order = jnp.argsort(scores, axis=-1)[:, :, :REPS * SLOTS].astype(jnp.int32)
    order = order.reshape(NBLK, NBLK, REPS, SLOTS)
    return jnp.transpose(order, (0, 2, 1, 3))


def draw_tile_rows(key, part):
    return (tile_positions(key) // RT).astype(jnp.int32)


def draw_tile_cols(key, part):
    return (tile_positions(key) % RT).astype(jnp.int32)


def draw_tile_counts(key, part):
    key = jax.random.fold_in(key, 11)
    first_key, second_key, third_key = jax.random.split(key, 3)
    column_level = jax.random.randint(first_key, (1, 1, NBLK), 0, 5)
    coins = jax.random.randint(second_key, (NBLK, REPS, NBLK), 0, 8)
    raw_counts = jnp.where(coins < column_level, SLOTS, 0)
    picked = jax.random.randint(third_key, (NBLK, REPS, 1), 0, NBLK)
    column_iota = jnp.arange(NBLK, dtype=jnp.int32)[None, None, :]
    return jnp.where(column_iota == picked, SLOTS, raw_counts).astype(jnp.int32)


def spiked(drawn, stream_key, source, target, shards_of, factor):
    owner, partner = [(jnp.arange(drawn.shape[position]) // (drawn.shape[position] // shards_of)).reshape([-1 if axis == position else 1 for axis in range(drawn.ndim)]) for position in (source, target)]
    chosen = jax.random.permutation(stream_key, shards_of)[partner]
    strong = (owner == chosen) | (owner == (partner + shards_of // 2) % shards_of)
    return jnp.where(strong, factor * drawn, drawn)


def level_of(rng, extent, cuts, low, top_value):
    level, own = 1.0, jax.random.fold_in(rng, 6)
    for axis_at, shards_of in cuts:
        draws = jnp.exp(jax.random.uniform(jax.random.fold_in(own, axis_at), (shards_of,), jnp.float32, low / len(cuts), top_value / len(cuts)))
        level = level * jnp.repeat(draws, extent[axis_at] // shards_of).reshape([-1 if axis == axis_at else 1 for axis in range(len(extent))])
    return level


def centred(key, extent, scale, most, cuts=(), kind=jnp.bfloat16):
    drawn = jax.random.normal(key, extent, jnp.float32) * scale
    if len(cuts) > 0:
        drawn = level_of(key, extent, cuts, -0.22, 0.18) * drawn
    return jnp.clip(drawn, min=-most, max=most).astype(kind)


def gaussian_with(key, shape, spread, limit, cuts, heavy, held_as=jnp.bfloat16):
    result = spread * jax.random.normal(key, shape, jnp.float32)
    if cuts:
        result = result * level_of(key, shape, cuts, -0.22, 0.18)
    return jnp.clip(spiked(result, jax.random.fold_in(key, 3), *heavy), -limit, limit).astype(held_as)


def setup_inputs(seed: int = 0) -> dict:
    seeds = jax.random.split(jax.random.key(seed), 8)
    return {
        "tile_values": gaussian_with(seeds[0], (NBLK, REPS, NBLK, SLOTS, TILE, TILE), (TILE * N_BLK // 2) ** -0.5, 0.1875, ((0, 32), (1, 4)), (0, 2, 32, 2.75)),
        "tile_rows": draw_tile_rows(jax.random.fold_in(seeds[7], 71), 0),
        "tile_cols": draw_tile_cols(jax.random.fold_in(seeds[7], 71), 0),
        "tile_counts": draw_tile_counts(jax.random.fold_in(seeds[7], 71), 0),
        "grad_out": centred(seeds[4], (NODES, F), 1.0, 6.0, ((0, 32),)),
        "features": centred(seeds[5], (NODES, DIN), (NODES ** -0.5), 0.125, ((0, 128),)),
        "weight": centred(seeds[6], (DIN, F), F ** -0.5, 0.25),
    }


def reference(tile_values, tile_rows, tile_cols, tile_counts, grad_out, features, weight):
    per_row = BLK_NODES // TILE
    g_tiles = grad_out.reshape(NBLK, per_row, TILE, F)

    def row_block(total, inputs):
        values_here, row_idx, col_idx, count_here, g_own = inputs
        selected = g_own[row_idx]
        product = jnp.einsum("rjsab,rjsaf->rjsbf", values_here.astype(jnp.float32), selected.astype(jnp.float32))
        valid = (jnp.arange(SLOTS)[None, None, :] < count_here[:, :, None]).astype(jnp.float32)
        place = (col_idx[..., None] == jnp.arange(per_row)[None, None, None, :]).astype(jnp.float32) * valid[..., None]
        term = jnp.einsum("rjsc,rjsbf->jcbf", place, product, precision=lax.Precision.HIGHEST)
        return total + term, None

    start_total = jnp.zeros((NBLK, per_row, TILE, F), jnp.float32)
    total, unused = lax.scan(row_block, start_total, (tile_values, tile_rows, tile_cols, tile_counts, g_tiles))
    rounded = total.reshape(NODES, F).astype(jnp.bfloat16)
    grad_features = jnp.dot(rounded, weight.T, preferred_element_type=jnp.float32)
    grad_weight = jnp.dot(features.T, rounded, preferred_element_type=jnp.float32)
    return grad_features, grad_weight
```

```python
import functools

import jax
import jax.numpy as jnp
from jax import lax
from jax.experimental import pallas as pl
from jax.experimental.pallas import tpu as pltpu
from jax.sharding import PartitionSpec as P

MESH = pl.DeviceIdType.MESH
F32 = jnp.float32
BF16 = jnp.bfloat16

ROWS = (176, 176, 160)
FIRST = (0, 176, 352)
X, Y, Z = 0, 1, 2
ORDERS = ((X, Z, Y), (Y, X, Z), (Z, Y, X))
QUARTER = (24, 24, 16)
QFIRST = (0, 96, 192)
GROUPS = ((0, 8), (8, 6), (14, 9), (23, 9))


def place(group, i):
    if group == 0:
        return 2, i // 2, i % 2
    if group == 1:
        return (i // 2 + 3) % 4, 2, i % 2
    return (i // 3 + 3) % 4, (i % 3 + 3) % 4, group - 2


def kernel(code_ref, tiles_ref, g_ref, x_ref, w_ref, gf_ref, gw_ref, *scratch):
    (t0, t1, code1, gt, xt, *rest) = scratch
    send = rest[0:3]
    full = rest[3:6]
    ra_m, ra_p, rb_m, rb_p = rest[6:9], rest[9:12], rest[12:15], rest[15:18]
    r2am, r2ap, r2bm, r2bp, r2fm, r2fp = (rest[18 + 3 * n : 21 + 3 * n] for n in range(6))
    r3am, r3ap, r3bm, r3bp, r3fm, r3fp = (rest[36 + 3 * n : 39 + 3 * n] for n in range(6))
    tot, gw, gwr, half, halfr = rest[54:59]
    x1, x2, x3 = rest[59:62], rest[62:65], rest[65:68]
    (tl, ts, tr, cs, cr, s1, ra, rb, s2, r2, s3, r3, es, er, xs, xr) = rest[68:]

    blk = lax.axis_index("blk")
    rep = lax.axis_index("rep")
    core = rep % 2
    pos = (blk // 8, (blk // 2) % 4, (rep // 2) * 2 + blk % 2)

    def device(where, which):
        return (where[0] * 8 + where[1] * 2 + where[2] % 2, (where[2] // 2) * 2 + which)

    def beside(axis, step):
        where = list(pos)
        where[axis] = (pos[axis] + step) % 4
        return device(where, core)

    partner = device(pos, 1 - core)

    def remote(src, dst, ssem, rsem, to):
        pltpu.make_async_remote_copy(
            src_ref=src, dst_ref=dst, send_sem=ssem, recv_sem=rsem, device_id=to, device_id_type=MESH
        ).start()

    def wait(ref, sem):
        pltpu.make_async_copy(ref, ref, sem).wait()

    def column(group, i):
        dx, dy, dl = place(group, i)
        return ((pos[0] + dx) % 4) * 8 + ((pos[1] + dy) % 4) * 2 + (pos[2] + dl) % 2

    mine = pl.ds(pl.multiple_of(core * 128, 128), 128)
    other = pl.ds(pl.multiple_of((1 - core) * 128, 128), 128)

    for group, (first, count) in enumerate(GROUPS):

        def load(i, carry, group=group, first=first):
            c = column(group, i)
            pltpu.make_async_copy(tiles_ref.at[c, :, mine], t0.at[first + i], tl.at[group]).start()
            return carry

        lax.fori_loop(0, count, load, 0)

    barrier = pltpu.get_barrier_semaphore()
    pl.semaphore_signal(barrier, inc=1, device_id=partner, device_id_type=MESH)
    for axis in (X, Y, Z):
        for step in (1, 2, 3):
            pl.semaphore_signal(barrier, inc=1, device_id=beside(axis, step), device_id_type=MESH)
    pl.semaphore_wait(barrier, 10)

    remote(code_ref, code1, cs, cr, partner)
    for group, (first, count) in enumerate(GROUPS):

        def swap(i, carry, group=group, first=first):
            c = column(group, i)
            remote(tiles_ref.at[c, :, other], t1.at[first + i], ts.at[group], tr.at[group], partner)
            return carry

        lax.fori_loop(0, count, swap, 0)

    gt[...] = g_ref[...].T
    xt[...] = x_ref[...].T
    wait(code1, cr)

    def products(group):
        first, count = GROUPS[group]
        wait(t0.at[first : first + count], tl.at[group])
        wait(t1.at[first : first + count], tr.at[group])

        def one(i, carry):
            dx, dy, dl = place(group, i)
            c = column(group, i)
            near = ((pos[2] + dl) % 4) // 2
            own, theirs = t0[first + i], t1[first + i]
            code_own = code_ref[pl.ds(c, 1), :]
            code_theirs = code1[pl.ds(c, 1), :]
            lines = []
            for row in range(2):
                line = []
                for col in (near, 1 - near):
                    key = (row * 2 + col).astype(F32)
                    keep_own = jnp.where(code_own == key, 1.0, 0.0).astype(BF16)
                    keep_theirs = jnp.where(code_theirs == key, 1.0, 0.0).astype(BF16)
                    line.append(own * keep_own + theirs * keep_theirs)
                lines.append(jnp.concatenate(line, axis=1))
            dense = jnp.concatenate(lines, axis=0)
            made = jnp.dot(gt[...], dense, preferred_element_type=F32)
            for part in range(3):
                rows = slice(FIRST[part], FIRST[part] + ROWS[part])
                for side in range(2):
                    block = made[rows, side * 128 : (side + 1) * 128]
                    rel = (dx, dy, dl + 2 * side)
                    at = tuple(rel[axis] for axis in ORDERS[part])
                    full[part][at] = block
                    send[part][at] = block.astype(BF16)
            return carry

        lax.fori_loop(0, count, one, 0)

    CHUNKS = (2, 1, 3, 0)

    def opposite1(part):
        axis = ORDERS[part][0]
        for t in CHUNKS:
            remote(send[part].at[2, t, 0:2], ra_m[part].at[t], s1.at[part, 0], ra.at[part, 0, t], beside(axis, 1))
            remote(send[part].at[2, t, 2:4], ra_p[part].at[t], s1.at[part, 0], ra.at[part, 1, t], beside(axis, 3))

    def plain1(part, t):
        axis = ORDERS[part][0]
        remote(send[part].at[1, t, 2:4], rb_m[part].at[t, 2:4], s1.at[part, 1], rb.at[part, 0, t], beside(axis, 1))
        remote(send[part].at[3, t, 0:2], rb_p[part].at[t, 0:2], s1.at[part, 2], rb.at[part, 1, t], beside(axis, 3))

    def merge1(part, t):
        axis = ORDERS[part][0]
        wait(ra_m[part].at[t], ra.at[part, 0, t])
        for b in range(2):
            send[part][1, t, b] = (full[part][1, t, b] + ra_m[part][t, b].astype(F32)).astype(BF16)
        remote(send[part].at[1, t, 0:2], rb_m[part].at[t, 0:2], s1.at[part, 1], rb.at[part, 0, t], beside(axis, 1))
        wait(ra_p[part].at[t], ra.at[part, 1, t])
        for b in range(2):
            send[part][3, t, 2 + b] = (full[part][3, t, 2 + b] + ra_p[part][t, b].astype(F32)).astype(BF16)
        remote(send[part].at[3, t, 2:4], rb_p[part].at[t, 2:4], s1.at[part, 2], rb.at[part, 1, t], beside(axis, 3))

    def sum1(part, t):
        wait(rb_m[part].at[t], rb.at[part, 0, t])
        wait(rb_p[part].at[t], rb.at[part, 1, t])

        def add(b, carry):
            total = full[part][0, t, b] + rb_m[part][t, b].astype(F32) + rb_p[part][t, b].astype(F32)
            full[part][0, t, b] = total
            send[part][0, t, b] = total.astype(BF16)
            return carry

        lax.fori_loop(0, 4, add, 0)

    products(0)
    opposite1(0)
    products(1)
    opposite1(1)
    products(2)
    opposite1(2)
    products(3)
    for t in CHUNKS:
        for part in range(3):
            plain1(part, t)
    for t in CHUNKS:
        for part in range(3):
            merge1(part, t)

    def merge2(part):
        axis = ORDERS[part][1]
        wait(r2am[part], r2.at[part, 0])
        for b in range(2):
            full[part][0, 1, b] = full[part][0, 1, b] + r2am[part][b].astype(F32)
        remote(full[part].at[0, 1, 0:2], r2fm[part], s2.at[part, 3], r2.at[part, 4], beside(axis, 1))
        wait(r2ap[part], r2.at[part, 1])
        for b in range(2):
            full[part][0, 3, 2 + b] = full[part][0, 3, 2 + b] + r2ap[part][b].astype(F32)
        remote(full[part].at[0, 3, 2:4], r2fp[part], s2.at[part, 4], r2.at[part, 5], beside(axis, 3))

    for t in CHUNKS:
        for part in range(3):
            axis = ORDERS[part][1]
            sum1(part, t)
            if t == 2:
                remote(send[part].at[0, 2, 0:2], r2am[part], s2.at[part, 0], r2.at[part, 0], beside(axis, 1))
                remote(send[part].at[0, 2, 2:4], r2ap[part], s2.at[part, 0], r2.at[part, 1], beside(axis, 3))
            if t == 1:
                remote(send[part].at[0, 1, 2:4], r2bm[part], s2.at[part, 1], r2.at[part, 2], beside(axis, 1))
            if t == 3:
                remote(send[part].at[0, 3, 0:2], r2bp[part], s2.at[part, 2], r2.at[part, 3], beside(axis, 3))
                merge2(part)

    for part in range(3):
        axis = ORDERS[part][2]
        mid, end = ROWS[part] // 2, ROWS[part]
        wait(r2fm[part], r2.at[part, 4])
        wait(r2bp[part], r2.at[part, 3])
        wait(r2bm[part], r2.at[part, 2])
        wait(r2fp[part], r2.at[part, 5])
        for b in (2, 1, 3, 0):
            if b < 2:
                arrived = r2fm[part][b] + r2bp[part][b].astype(F32)
            else:
                arrived = r2bm[part][b - 2].astype(F32) + r2fp[part][b - 2]
            full[part][0, 0, b] = full[part][0, 0, b] + arrived
            if b == 2:
                remote(full[part].at[0, 0, 2, 0:mid], r3am[part], s3.at[part, 0], r3.at[part, 0], beside(axis, 1))
                remote(full[part].at[0, 0, 2, mid:end], r3ap[part], s3.at[part, 1], r3.at[part, 1], beside(axis, 3))
            if b == 1:
                remote(full[part].at[0, 0, 1, mid:end], r3bm[part], s3.at[part, 2], r3.at[part, 2], beside(axis, 1))
            if b == 3:
                remote(full[part].at[0, 0, 3, 0:mid], r3bp[part], s3.at[part, 3], r3.at[part, 3], beside(axis, 3))
    for part in range(3):
        axis = ORDERS[part][2]
        mid, end = ROWS[part] // 2, ROWS[part]
        wait(r3am[part], r3.at[part, 0])
        full[part][0, 0, 1, 0:mid] = full[part][0, 0, 1, 0:mid] + r3am[part][...]
        remote(full[part].at[0, 0, 1, 0:mid], r3fm[part], s3.at[part, 4], r3.at[part, 4], beside(axis, 1))
        wait(r3ap[part], r3.at[part, 1])
        full[part][0, 0, 3, mid:end] = full[part][0, 0, 3, mid:end] + r3ap[part][...]
        remote(full[part].at[0, 0, 3, mid:end], r3fp[part], s3.at[part, 5], r3.at[part, 5], beside(axis, 3))
    for part in range(3):
        mid, end = ROWS[part] // 2, ROWS[part]
        at = FIRST[part]
        wait(r3bp[part], r3.at[part, 3])
        wait(r3fm[part], r3.at[part, 4])
        tot[at : at + mid] = full[part][0, 0, 0, 0:mid] + r3fm[part][...] + r3bp[part][...]
        wait(r3bm[part], r3.at[part, 2])
        wait(r3fp[part], r3.at[part, 5])
        tot[at + mid : at + end] = full[part][0, 0, 0, mid:end] + r3bm[part][...] + r3fp[part][...]

    total = tot[...].T
    high = total.astype(BF16)
    low = (total - high.astype(F32)).astype(BF16)

    gw[...] = jnp.dot(xt[...], high, preferred_element_type=F32) + jnp.dot(xt[...], low, preferred_element_type=F32)
    kept = pl.ds(pl.multiple_of(core * 256, 256), 256)
    given = pl.ds(pl.multiple_of((1 - core) * 256, 256), 256)
    remote(gw.at[given], gwr, es.at[0], er.at[0], partner)
    last = (((1,), (1,)), ((), ()))
    gf_ref[...] = lax.dot_general(high, w_ref[...], last, preferred_element_type=F32) + lax.dot_general(
        low, w_ref[...], last, preferred_element_type=F32
    )
    wait(gwr, er.at[0])
    half[...] = gw[kept, :] + gwr[...]

    for part in range(3):
        axis, size = ORDERS[part][0], QUARTER[part]
        for step in (2, 1, 3):
            quarter = pl.ds(pl.multiple_of(QFIRST[part] + ((pos[axis] + step) % 4) * size, 8), size)
            remote(half.at[quarter], x1[part].at[pos[axis]], xs.at[0, part], xr.at[0, part], beside(axis, step))
        x1[part][pos[axis]] = half[pl.ds(pl.multiple_of(QFIRST[part] + pos[axis] * size, 8), size), :]
    for stage, (took, gave) in enumerate(((x1, x2), (x2, x3))):
        for part in range(3):
            axis = ORDERS[part][stage + 1]
            wait(took[part].at[0:3], xr.at[stage, part])
            gave[part][pos[axis]] = (took[part][0] + took[part][1]) + (took[part][2] + took[part][3])
            for step in (2, 1, 3):
                here = gave[part].at[pos[axis]]
                remote(here, here, xs.at[stage + 1, part], xr.at[stage + 1, part], beside(axis, step))
    for part in range(3):
        axis, size = ORDERS[part][0], QUARTER[part]
        wait(x3[part].at[0:3], xr.at[2, part])
        wait(x1[part].at[0:3], xs.at[0, part])
        gwr[pl.ds(pl.multiple_of(QFIRST[part] + pos[axis] * size, 8), size), :] = (x3[part][0] + x3[part][1]) + (
            x3[part][2] + x3[part][3]
        )
        quarter = gwr.at[pl.ds(pl.multiple_of(QFIRST[part] + pos[axis] * size, 8), size)]
        for step in (2, 1, 3):
            remote(quarter, quarter, xs.at[3, part], xr.at[3, part], beside(axis, step))
    wait(gw.at[given], es.at[0])
    for part in range(3):
        size = QUARTER[part]
        wait(gwr.at[QFIRST[part] : QFIRST[part] + 3 * size], xr.at[3, part])
        rows = slice(QFIRST[part], QFIRST[part] + 4 * size)
        remote(gwr.at[rows], halfr.at[rows], es.at[1 + part], er.at[1 + part], partner)
    gw_ref[kept, :] = gwr[...]
    for part in range(3):
        size = QUARTER[part]
        rows = slice(QFIRST[part], QFIRST[part] + 4 * size)
        wait(halfr.at[rows], er.at[1 + part])
    gw_ref[given, :] = halfr[...]

    wait(code_ref, cs)
    for group, (first, count) in enumerate(GROUPS):
        wait(t1.at[first : first + count], ts.at[group])
    for part in range(3):
        mid, end = ROWS[part] // 2, ROWS[part]
        for n, region in enumerate((2, 1, 3)):
            wait(send[part].at[region], s1.at[part, n])
        wait(send[part].at[0, 2], s2.at[part, 0])
        wait(send[part].at[0, 1, 2:4], s2.at[part, 1])
        wait(send[part].at[0, 3, 0:2], s2.at[part, 2])
        wait(full[part].at[0, 1, 0:2], s2.at[part, 3])
        wait(full[part].at[0, 3, 2:4], s2.at[part, 4])
        for n in range(6):
            wait(r3am[part], s3.at[part, n])
        for stage in (1, 2):
            wait(x2[part].at[0:3], xs.at[stage, part])
        size = QUARTER[part]
        wait(gwr.at[QFIRST[part] : QFIRST[part] + 3 * size], xs.at[3, part])
        rows = slice(QFIRST[part], QFIRST[part] + 4 * size)
        wait(gwr.at[rows], es.at[1 + part])


def body(tile_values, tile_rows, tile_cols, tile_counts, grad_out, features, weight):
    tiles = tile_values[0, 0, :, 0]
    spot = tile_rows[0, 0, :, 0] * 2 + tile_cols[0, 0, :, 0]
    code = jnp.where(tile_counts[0, 0] > 0, spot, -1).astype(F32)
    code = jnp.broadcast_to(code[:, None], (32, 128))
    vmem = pl.BlockSpec(memory_space=pltpu.VMEM)

    def per_part(*shape, dtype, rows=ROWS, lanes=128):
        return [pltpu.VMEM((*shape, r, lanes), dtype) for r in rows]

    halves = tuple(r // 2 for r in ROWS)
    dma = pltpu.SemaphoreType.DMA
    scratch = [
        pltpu.VMEM((32, 256, 128), BF16),
        pltpu.VMEM((32, 256, 128), BF16),
        pltpu.VMEM((32, 128), F32),
        pltpu.VMEM((512, 512), BF16),
        pltpu.VMEM((512, 128), BF16),
        *per_part(4, 4, 4, dtype=BF16),
        *per_part(4, 4, 4, dtype=F32),
        *per_part(4, 2, dtype=BF16),
        *per_part(4, 2, dtype=BF16),
        *per_part(4, 4, dtype=BF16),
        *per_part(4, 4, dtype=BF16),
        *per_part(2, dtype=BF16),
        *per_part(2, dtype=BF16),
        *per_part(2, dtype=BF16),
        *per_part(2, dtype=BF16),
        *per_part(2, dtype=F32),
        *per_part(2, dtype=F32),
    ]
    for _ in range(6):
        scratch += per_part(dtype=F32, rows=halves)
    scratch += [
        pltpu.VMEM((512, 128), F32),
        pltpu.VMEM((512, 512), F32),
        pltpu.VMEM((256, 512), F32),
        pltpu.VMEM((256, 512), F32),
        pltpu.VMEM((256, 512), F32),
    ]
    for _ in range(3):
        scratch += per_part(4, dtype=F32, rows=QUARTER, lanes=512)
    scratch += [
        dma((4,)),
        dma((4,)),
        dma((4,)),
        dma,
        dma,
        dma((3, 3)),
        dma((3, 2, 4)),
        dma((3, 2, 4)),
        dma((3, 5)),
        dma((3, 6)),
        dma((3, 6)),
        dma((3, 6)),
        dma((4,)),
        dma((4,)),
        dma((4, 3)),
        dma((4, 3)),
    ]
    return pl.pallas_call(
        kernel,
        out_shape=(jax.ShapeDtypeStruct((128, 512), F32), jax.ShapeDtypeStruct((512, 512), F32)),
        in_specs=[vmem, pl.BlockSpec(memory_space=pl.ANY), vmem, vmem, vmem],
        out_specs=(vmem, vmem),
        scratch_shapes=scratch,
        compiler_params=pltpu.CompilerParams(
            collective_id=0, has_side_effects=True, vmem_limit_bytes=56 * 1024 * 1024
        ),
    )(code, tiles, grad_out, features, weight)


def solution(mesh):
    placed = (
        P("blk", "rep", None, None, None, None),
        P("blk", "rep", None, None),
        P("blk", "rep", None, None),
        P("blk", "rep", None),
        P("blk", None),
        P(("blk", "rep"), None),
        P(),
    )
    return jax.shard_map(
        body, mesh=mesh, in_specs=placed, out_specs=(P(("blk", "rep"), None), P()), check_vma=False
    )
```

```python
import functools

import jax
import jax.numpy as jnp
from jax import lax
from jax.experimental import pallas as pl
from jax.experimental.pallas import tpu as pltpu
from jax.sharding import PartitionSpec as P

MESH = pl.DeviceIdType.MESH
F32 = jnp.float32
BF16 = jnp.bfloat16

ROWS = (176, 176, 160)
FIRST = (0, 176, 352)
X, Y, Z = 0, 1, 2
ORDERS = ((X, Z, Y), (Y, X, Z), (Z, Y, X))
QUARTER = (24, 24, 16)
QFIRST = (0, 96, 192)
GROUPS = ((0, 8), (8, 6), (14, 9), (23, 9))


def place(group, i):
    if group == 0:
        return 2, (i // 2 + 2) % 4, i % 2
    if group == 1:
        return (i // 2 + 3) % 4, 2, i % 2
    return (i // 3 + 3) % 4, (i % 3 + 3) % 4, group - 2


def kernel(rows_ref, cols_ref, counts_ref, tiles_ref, g_any, x_any, w_any, gf_any, gw_any, *scratch):
    (t0, t1, code0, code1, g_ref, x_ref, w_ref, gf, gt, xt, *rest) = scratch
    send = rest[0:3]
    full = rest[3:6]
    ra, rb = rest[6:9], rest[9:12]
    r2am, r2ap, r2bm, r2bp, r2fm, r2fp = (rest[12 + 3 * n : 15 + 3 * n] for n in range(6))
    r3am, r3ap, r3bm, r3bp, r3fm, r3fp = (rest[30 + 3 * n : 33 + 3 * n] for n in range(6))
    tot, gw, gwr, half, halfr, halfp = rest[48:54]
    x1, x2, x3 = rest[54:57], rest[57:60], rest[60:63]
    (ins, outs, tl, ts, tr, cs, cr, s1, ras, rbs, s2, r2, s3, r3, es, er, xs, xr, fs, fr) = rest[63:]

    blk = lax.axis_index("blk")
    rep = lax.axis_index("rep")
    core = rep % 2
    pos = (blk // 8, (blk // 2) % 4, (rep // 2) * 2 + blk % 2)

    def device(where, which):
        return (where[0] * 8 + where[1] * 2 + where[2] % 2, (where[2] // 2) * 2 + which)

    def beside(axis, step):
        where = list(pos)
        where[axis] = (pos[axis] + step) % 4
        return device(where, core)

    partner = device(pos, 1 - core)

    def remote(src, dst, ssem, rsem, to):
        pltpu.make_async_remote_copy(
            src_ref=src, dst_ref=dst, send_sem=ssem, recv_sem=rsem, device_id=to, device_id_type=MESH
        ).start()

    def wait(ref, sem):
        pltpu.make_async_copy(ref, ref, sem).wait()

    def column(group, i):
        dx, dy, dl = place(group, i)
        return ((pos[0] + dx) % 4) * 8 + ((pos[1] + dy) % 4) * 2 + (pos[2] + dl) % 2

    mine = pl.ds(pl.multiple_of(core * 128, 128), 128)
    other = pl.ds(pl.multiple_of((1 - core) * 128, 128), 128)

    for group, (first, count) in enumerate(GROUPS):

        def load(i, carry, group=group, first=first):
            c = column(group, i)
            pltpu.make_async_copy(tiles_ref.at[c, :, mine], t0.at[first + i], tl.at[group]).start()
            return carry

        lax.fori_loop(0, count, load, 0)

    def fetch(src, dst, sem):
        copy = pltpu.make_async_copy(src, dst, sem)
        copy.start()
        return copy

    get_g = fetch(g_any, g_ref, ins.at[0])
    get_x = fetch(x_any, x_ref, ins.at[1])
    get_w = fetch(w_any, w_ref, ins.at[2])

    sent = []

    def finish():
        for region, sem in sent:
            wait(region, sem)

    barrier = pltpu.get_barrier_semaphore()
    pl.semaphore_signal(barrier, inc=1, device_id=partner, device_id_type=MESH)
    for axis in (X, Y, Z):
        for step in (1, 2, 3):
            pl.semaphore_signal(barrier, inc=1, device_id=beside(axis, step), device_id_type=MESH)
    for c in range(32):
        spot = rows_ref[0, 0, c] * 2 + cols_ref[0, 0, c]
        used = jnp.where(counts_ref[0, 0, c] > 0, spot, -1)
        code0[c : c + 1, :] = jnp.full((1, 128), used, jnp.int32).astype(F32)
    get_g.wait()
    gt[...] = g_ref[...].T
    pl.semaphore_wait(barrier, 10)

    remote(code0, code1, cs, cr, partner)
    sent.append((code0, cs))
    for group, (first, count) in enumerate(GROUPS):

        def swap(i, carry, group=group, first=first):
            c = column(group, i)
            remote(tiles_ref.at[c, :, other], t1.at[first + i], ts.at[group], tr.at[group], partner)
            return carry

        lax.fori_loop(0, count, swap, 0)
        sent.append((t1.at[first : first + count], ts.at[group]))

    get_x.wait()
    xt[...] = x_ref[...].T
    wait(code1, cr)

    def send1(part, at1, at2, at3):
        axis = ORDERS[part][0]
        opposite = (at1 // 2) * (1 - at1 % 2)
        way = opposite * (at3 // 2) + (1 - opposite) * (at1 // 2)
        plain = (at1 % 2) * ((at1 // 2 + at3 // 2) % 2)
        block = send[part].at[at1, at2, at3]
        to = beside(axis, 1 + 2 * way)

        @pl.when(opposite == 1)
        def _():
            remote(block, ra[part].at[way, at2, at3 % 2], s1.at[part, at1], ras.at[part, way, at2], to)

        @pl.when(plain == 1)
        def _():
            remote(block, rb[part].at[way, at2, at3], s1.at[part, at1], rbs.at[part, way, at2], to)

    def products(group):
        first, count = GROUPS[group]
        wait(t0.at[first : first + count], tl.at[group])
        wait(t1.at[first : first + count], tr.at[group])

        def one(i, carry):
            dx, dy, dl = place(group, i)
            c = column(group, i)
            near = ((pos[2] + dl) % 4) // 2
            own, theirs = t0[first + i], t1[first + i]
            code_own = code0[pl.ds(c, 1), :]
            code_theirs = code1[pl.ds(c, 1), :]
            lines = []
            for row in range(2):
                line = []
                for col in (near, 1 - near):
                    key = (row * 2 + col).astype(F32)
                    keep_own = jnp.where(code_own == key, 1.0, 0.0).astype(BF16)
                    keep_theirs = jnp.where(code_theirs == key, 1.0, 0.0).astype(BF16)
                    line.append(own * keep_own + theirs * keep_theirs)
                lines.append(jnp.concatenate(line, axis=1))
            dense = jnp.concatenate(lines, axis=0)
            made = jnp.dot(gt[...], dense, preferred_element_type=F32)
            for part in range(3):
                rows = slice(FIRST[part], FIRST[part] + ROWS[part])
                for side in range(2):
                    block = made[rows, side * 128 : (side + 1) * 128]
                    rel = (dx, dy, dl + 2 * side)
                    at = tuple(rel[axis] for axis in ORDERS[part])
                    full[part][at] = block
                    send[part][at] = block.astype(BF16)
            for part in range(3):
                for side in range(2):
                    rel = (dx, dy, dl + 2 * side)
                    send1(part, *(rel[axis] for axis in ORDERS[part]))
            return carry

        lax.fori_loop(0, count, one, 0)

    def merge1(part, t):
        axis = ORDERS[part][0]
        for way, at1, low in ((0, 1, 0), (1, 3, 2)):
            wait(ra[part].at[way, t], ras.at[part, way, t])
            for b in range(2):
                send[part][at1, t, low + b] = (full[part][at1, t, low + b] + ra[part][way, t, b].astype(F32)).astype(BF16)
            pair = slice(low, low + 2)
            remote(
                send[part].at[at1, t, pair],
                rb[part].at[way, t, pair],
                s1.at[part, at1],
                rbs.at[part, way, t],
                beside(axis, 1 + 2 * way),
            )

    def sum1(part, t):
        wait(rb[part].at[0, t], rbs.at[part, 0, t])
        wait(rb[part].at[1, t], rbs.at[part, 1, t])

        def add(b, carry):
            total = full[part][0, t, b] + rb[part][0, t, b].astype(F32) + rb[part][1, t, b].astype(F32)
            full[part][0, t, b] = total
            send[part][0, t, b] = total.astype(BF16)
            return carry

        lax.fori_loop(0, 4, add, 0)

    def merge2(part):
        axis = ORDERS[part][1]
        wait(r2am[part], r2.at[part, 0])
        for b in range(2):
            full[part][0, 1, b] = full[part][0, 1, b] + r2am[part][b].astype(F32)
        remote(full[part].at[0, 1, 0:2], r2fm[part], s2.at[part, 3], r2.at[part, 4], beside(axis, 1))
        wait(r2ap[part], r2.at[part, 1])
        for b in range(2):
            full[part][0, 3, 2 + b] = full[part][0, 3, 2 + b] + r2ap[part][b].astype(F32)
        remote(full[part].at[0, 3, 2:4], r2fp[part], s2.at[part, 4], r2.at[part, 5], beside(axis, 3))

    def step2(part, t):
        axis = ORDERS[part][1]
        sum1(part, t)
        if t == 2:
            remote(send[part].at[0, 2, 0:2], r2am[part], s2.at[part, 0], r2.at[part, 0], beside(axis, 1))
            remote(send[part].at[0, 2, 2:4], r2ap[part], s2.at[part, 0], r2.at[part, 1], beside(axis, 3))
        if t == 1:
            remote(send[part].at[0, 1, 2:4], r2bm[part], s2.at[part, 1], r2.at[part, 2], beside(axis, 1))
        if t == 3:
            remote(send[part].at[0, 3, 0:2], r2bp[part], s2.at[part, 2], r2.at[part, 3], beside(axis, 3))

    products(0)
    products(1)
    merge1(1, 2)
    products(2)
    merge1(2, 2)
    merge1(0, 2)
    products(3)
    for t in (1, 3):
        for part in (1, 2, 0):
            merge1(part, t)
    for part in (1, 2, 0):
        step2(part, 2)
        merge1(part, 0)
    for part in (1, 2, 0):
        step2(part, 1)
    for part in (1, 2, 0):
        step2(part, 3)
        merge2(part)
    for part in (1, 2, 0):
        step2(part, 0)
    for part in range(3):
        for at1 in (1, 2, 3):
            sent.append((send[part].at[at1], s1.at[part, at1]))
        sent.append((send[part].at[0, 2], s2.at[part, 0]))
        sent.append((send[part].at[0, 1, 2:4], s2.at[part, 1]))
        sent.append((send[part].at[0, 3, 0:2], s2.at[part, 2]))
        sent.append((full[part].at[0, 1, 0:2], s2.at[part, 3]))
        sent.append((full[part].at[0, 3, 2:4], s2.at[part, 4]))

    for part in range(3):
        axis = ORDERS[part][2]
        mid, end = ROWS[part] // 2, ROWS[part]
        wait(r2fm[part], r2.at[part, 4])
        wait(r2bp[part], r2.at[part, 3])
        wait(r2bm[part], r2.at[part, 2])
        wait(r2fp[part], r2.at[part, 5])
        for b in (2, 1, 3, 0):
            if b < 2:
                arrived = r2fm[part][b] + r2bp[part][b].astype(F32)
            else:
                arrived = r2bm[part][b - 2].astype(F32) + r2fp[part][b - 2]
            full[part][0, 0, b] = full[part][0, 0, b] + arrived
            if b == 2:
                remote(full[part].at[0, 0, 2, 0:mid], r3am[part], s3.at[part, 0], r3.at[part, 0], beside(axis, 1))
                remote(full[part].at[0, 0, 2, mid:end], r3ap[part], s3.at[part, 1], r3.at[part, 1], beside(axis, 3))
            if b == 1:
                remote(full[part].at[0, 0, 1, mid:end], r3bm[part], s3.at[part, 2], r3.at[part, 2], beside(axis, 1))
            if b == 3:
                remote(full[part].at[0, 0, 3, 0:mid], r3bp[part], s3.at[part, 3], r3.at[part, 3], beside(axis, 3))
    for part in range(3):
        axis = ORDERS[part][2]
        mid, end = ROWS[part] // 2, ROWS[part]
        wait(r3am[part], r3.at[part, 0])
        full[part][0, 0, 1, 0:mid] = full[part][0, 0, 1, 0:mid] + r3am[part][...]
        remote(full[part].at[0, 0, 1, 0:mid], r3fm[part], s3.at[part, 4], r3.at[part, 4], beside(axis, 1))
        wait(r3ap[part], r3.at[part, 1])
        full[part][0, 0, 3, mid:end] = full[part][0, 0, 3, mid:end] + r3ap[part][...]
        remote(full[part].at[0, 0, 3, mid:end], r3fp[part], s3.at[part, 5], r3.at[part, 5], beside(axis, 3))
    for part in range(3):
        mid, end = ROWS[part] // 2, ROWS[part]
        at = FIRST[part]
        wait(r3bp[part], r3.at[part, 3])
        wait(r3fm[part], r3.at[part, 4])
        tot[at : at + mid] = full[part][0, 0, 0, 0:mid] + r3fm[part][...] + r3bp[part][...]
        wait(r3bm[part], r3.at[part, 2])
        wait(r3fp[part], r3.at[part, 5])
        tot[at + mid : at + end] = full[part][0, 0, 0, mid:end] + r3bm[part][...] + r3fp[part][...]

    for part in range(3):
        for n in range(6):
            sent.append((r3am[part], s3.at[part, n]))

    total = tot[...].T
    high = total.astype(BF16)
    low = (total - high.astype(F32)).astype(BF16)

    kept = pl.ds(pl.multiple_of(core * 256, 256), 256)
    given = pl.ds(pl.multiple_of((1 - core) * 256, 256), 256)
    for rows in (given, kept):
        left = xt[rows, :]
        gw[rows, :] = jnp.dot(left, high, preferred_element_type=F32) + jnp.dot(left, low, preferred_element_type=F32)
        if rows is given:
            remote(gw.at[given], gwr, es, er, partner)
    sent.append((gwr, es))
    wait(gwr, er)
    half[...] = gw[kept, :] + gwr[...]

    for part in range(3):
        axis, size = ORDERS[part][0], QUARTER[part]
        for step in (2, 1, 3):
            quarter = pl.ds(pl.multiple_of(QFIRST[part] + ((pos[axis] + step) % 4) * size, 8), size)
            remote(half.at[quarter], x1[part].at[pos[axis]], xs.at[0, part], xr.at[0, part], beside(axis, step))
        x1[part][pos[axis]] = half[pl.ds(pl.multiple_of(QFIRST[part] + pos[axis] * size, 8), size), :]
        sent.append((x1[part].at[0:3], xs.at[0, part]))
    get_w.wait()
    last = (((1,), (1,)), ((), ()))
    gf[...] = lax.dot_general(high, w_ref[...], last, preferred_element_type=F32) + lax.dot_general(
        low, w_ref[...], last, preferred_element_type=F32
    )
    out_f = fetch(gf, gf_any, outs.at[0])
    for part in range(3):
        axis = ORDERS[part][1]
        wait(x1[part].at[0:3], xr.at[0, part])
        x1[part][0] = (x1[part][0] + x1[part][1]) + (x1[part][2] + x1[part][3])
        for step in (2, 1, 3):
            lanes = pl.ds(pl.multiple_of(((pos[axis] + step) % 4) * 128, 128), 128)
            remote(x1[part].at[0, :, lanes], x2[part].at[pos[axis]], xs.at[1, part], xr.at[1, part], beside(axis, step))
        x2[part][pos[axis]] = x1[part][0, :, pl.ds(pl.multiple_of(pos[axis] * 128, 128), 128)]
        sent.append((x2[part].at[0:3], xs.at[1, part]))
    for part in range(3):
        axis = ORDERS[part][2]
        wait(x2[part].at[0:3], xr.at[1, part])
        x3[part][pos[axis]] = (x2[part][0] + x2[part][1]) + (x2[part][2] + x2[part][3])
        for step in (2, 1, 3):
            here = x3[part].at[pos[axis]]
            remote(here, here, xs.at[2, part], xr.at[2, part], beside(axis, step))
        sent.append((x3[part].at[0:3], xs.at[2, part]))
    for part in range(3):
        axis, size = ORDERS[part][1], QUARTER[part]
        wait(x3[part].at[0:3], xr.at[2, part])
        lanes = pl.ds(pl.multiple_of(pos[axis] * 128, 128), 128)
        rows = pl.ds(pl.multiple_of(QFIRST[part] + pos[ORDERS[part][0]] * size, 8), size)
        halfr[rows, lanes] = (x3[part][0] + x3[part][1]) + (x3[part][2] + x3[part][3])
        here = halfr.at[rows, lanes]
        for step in (2, 1, 3):
            remote(here, here, xs.at[3, part], xr.at[3, part], beside(axis, step))
        sent.append((x3[part].at[0:3], xs.at[3, part]))

    puts = []
    for part in range(3):
        axis, size = ORDERS[part][0], QUARTER[part]
        wait(x3[part].at[0:3], xr.at[3, part])
        rows = pl.ds(pl.multiple_of(QFIRST[part] + pos[axis] * size, 8), size)
        here = halfr.at[rows]
        for step in (2, 1, 3):
            remote(here, here, xs.at[4, part], xr.at[4, part], beside(axis, step))
        remote(here, halfp.at[rows], fs.at[0, part], fr.at[0, part], partner)
        sent.append((halfr.at[0 : 3 * size], xs.at[4, part]))
        sent.append((halfr.at[0:size], fs.at[0, part]))
    for part in range(3):
        axis, size = ORDERS[part][0], QUARTER[part]
        wait(halfr.at[0 : 3 * size], xr.at[4, part])
        for step in (1, 2, 3):
            rows = pl.ds(pl.multiple_of(QFIRST[part] + ((pos[axis] + step) % 4) * size, 8), size)
            remote(halfr.at[rows], halfp.at[rows], fs.at[1, part], fr.at[1, part], partner)
        sent.append((halfr.at[0 : 3 * size], fs.at[1, part]))
    puts.append(fetch(halfr, gw_any.at[kept], outs.at[1]))
    for part in range(3):
        size = QUARTER[part]
        wait(halfr.at[0:size], fr.at[0, part])
        wait(halfr.at[0 : 3 * size], fr.at[1, part])
    puts.append(fetch(halfp, gw_any.at[given], outs.at[2]))
    for put in puts:
        put.wait()
    out_f.wait()
    finish()


def deliver(gf_from, gw_from, gf_to, gw_to, gf, gw, ins, outs):
    pieces = [(gf_from, gf, gf_to)]
    for n in range(4):
        rows = pl.ds(128 * n, 128)
        pieces.append((gw_from.at[rows], gw.at[rows], gw_to.at[rows]))
    gets = [pltpu.make_async_copy(src, mid, ins.at[n]) for n, (src, mid, _) in enumerate(pieces)]
    puts = [pltpu.make_async_copy(mid, dst, outs.at[n]) for n, (_, mid, dst) in enumerate(pieces)]
    for get in gets:
        get.start()
    for get, put in zip(gets, puts):
        get.wait()
        put.start()
    for put in puts:
        put.wait()


def body(tile_values, tile_rows, tile_cols, tile_counts, grad_out, features, weight):
    tiles = tile_values[0, 0, :, 0]
    anywhere = pl.BlockSpec(memory_space=pl.ANY)
    smem = pl.BlockSpec(memory_space=pltpu.SMEM)

    def per_part(*shape, dtype, rows=ROWS, lanes=128):
        return [pltpu.VMEM((*shape, r, lanes), dtype) for r in rows]

    halves = tuple(r // 2 for r in ROWS)
    dma = pltpu.SemaphoreType.DMA
    scratch = [
        pltpu.VMEM((32, 256, 128), BF16),
        pltpu.VMEM((32, 256, 128), BF16),
        pltpu.VMEM((32, 128), F32),
        pltpu.VMEM((32, 128), F32),
        pltpu.VMEM((512, 512), BF16),
        pltpu.VMEM((128, 512), BF16),
        pltpu.VMEM((512, 512), BF16),
        pltpu.VMEM((128, 512), F32),
        pltpu.VMEM((512, 512), BF16),
        pltpu.VMEM((512, 128), BF16),
        *per_part(4, 4, 4, dtype=BF16),
        *per_part(4, 4, 4, dtype=F32),
        *per_part(2, 4, 2, dtype=BF16),
        *per_part(2, 4, 4, dtype=BF16),
        *per_part(2, dtype=BF16),
        *per_part(2, dtype=BF16),
        *per_part(2, dtype=BF16),
        *per_part(2, dtype=BF16),
        *per_part(2, dtype=F32),
        *per_part(2, dtype=F32),
    ]
    for _ in range(6):
        scratch += per_part(dtype=F32, rows=halves)
    scratch += [
        pltpu.VMEM((512, 128), F32),
        pltpu.VMEM((512, 512), F32),
        pltpu.VMEM((256, 512), F32),
        pltpu.VMEM((256, 512), F32),
        pltpu.VMEM((256, 512), F32),
        pltpu.VMEM((256, 512), F32),
    ]
    for lanes in (512, 128, 128):
        scratch += per_part(4, dtype=F32, rows=QUARTER, lanes=lanes)
    scratch += [
        dma((3,)),
        dma((3,)),
        dma((4,)),
        dma((4,)),
        dma((4,)),
        dma,
        dma,
        dma((3, 4)),
        dma((3, 2, 4)),
        dma((3, 2, 4)),
        dma((3, 5)),
        dma((3, 6)),
        dma((3, 6)),
        dma((3, 6)),
        dma,
        dma,
        dma((5, 3)),
        dma((5, 3)),
        dma((2, 3)),
        dma((2, 3)),
    ]
    outputs = (jax.ShapeDtypeStruct((128, 512), F32), jax.ShapeDtypeStruct((512, 512), F32))
    made = pl.pallas_call(
        kernel,
        out_shape=outputs,
        in_specs=[smem, smem, smem, anywhere, anywhere, anywhere, anywhere],
        out_specs=(anywhere, anywhere),
        scratch_shapes=scratch,
        compiler_params=pltpu.CompilerParams(
            collective_id=0, has_side_effects=True, vmem_limit_bytes=56 * 1024 * 1024
        ),
    )(tile_rows[..., 0], tile_cols[..., 0], tile_counts, tiles, grad_out, features, weight)
    return pl.pallas_call(
        deliver,
        out_shape=outputs,
        in_specs=[anywhere, anywhere],
        out_specs=(anywhere, anywhere),
        scratch_shapes=[pltpu.VMEM((128, 512), F32), pltpu.VMEM((512, 512), F32), dma((5,)), dma((5,))],
    )(*made)


def solution(mesh):
    placed = (
        P("blk", "rep", None, None, None, None),
        P("blk", "rep", None, None),
        P("blk", "rep", None, None),
        P("blk", "rep", None),
        P("blk", None),
        P(("blk", "rep"), None),
        P(),
    )
    return jax.shard_map(
        body, mesh=mesh, in_specs=placed, out_specs=(P(("blk", "rep"), None), P()), check_vma=False
    )
```

```python
import functools

import jax
import jax.numpy as jnp
from jax import lax
from jax.experimental import pallas as pl
from jax.experimental.pallas import tpu as pltpu
from jax.sharding import PartitionSpec as P

MESH = pl.DeviceIdType.MESH
F32 = jnp.float32
BF16 = jnp.bfloat16

ROWS = (176, 176, 160)
FIRST = (0, 176, 352)
X, Y, Z = 0, 1, 2
ORDERS = ((X, Z, Y), (Y, X, Z), (Z, Y, X))
QUARTER = (24, 24, 16)
QFIRST = (0, 96, 192)
GROUPS = ((0, 2), (2, 6), (8, 6), (14, 9), (23, 9))


def place(group, i):
    if group == 0:
        return 2, 2 + 0 * i, i
    if group == 1:
        return 2, (i // 2 + 3) % 4, i % 2
    if group == 2:
        return (i // 2 + 3) % 4, 2, i % 2
    return (i // 3 + 3) % 4, (i % 3 + 3) % 4, group - 3


def kernel(rows_ref, cols_ref, counts_ref, tiles_ref, g_any, x_any, w_any, gf, gw_out, *scratch):
    (t0, t1, code0, code1, g_ref, w_ref, gt, xg, *rest) = scratch
    send = rest[0:3]
    full = rest[3:6]
    ra, rb, rc, rd = rest[6:9], rest[9:12], rest[12:15], rest[15:18]
    tot, gw, gwr, half = rest[18:22]
    x1, x2, x3 = rest[22:25], rest[25:28], rest[28:31]
    (ins, gs, gr, tl, ts, tr, cs, cr, s1, ras, rbs, s2, r2, s3, r3, es, er, xs, xr, fs, fr) = rest[31:]

    blk = lax.axis_index("blk")
    rep = lax.axis_index("rep")
    core = rep % 2
    pos = (blk // 8, (blk // 2) % 4, (rep // 2) * 2 + blk % 2)

    def device(where, which):
        return (where[0] * 8 + where[1] * 2 + where[2] % 2, (where[2] // 2) * 2 + which)

    def beside(axis, step):
        where = list(pos)
        where[axis] = (pos[axis] + step) % 4
        return device(where, core)

    partner = device(pos, 1 - core)

    def remote(src, dst, ssem, rsem, to):
        pltpu.make_async_remote_copy(
            src_ref=src, dst_ref=dst, send_sem=ssem, recv_sem=rsem, device_id=to, device_id_type=MESH
        ).start()

    def wait(ref, sem):
        pltpu.make_async_copy(ref, ref, sem).wait()

    def column(group, i):
        dx, dy, dl = place(group, i)
        return ((pos[0] + dx) % 4) * 8 + ((pos[1] + dy) % 4) * 2 + (pos[2] + dl) % 2

    mine = pl.ds(pl.multiple_of(core * 128, 128), 128)
    other = pl.ds(pl.multiple_of((1 - core) * 128, 128), 128)

    for group, (first, count) in enumerate(GROUPS):

        def load(i, carry, group=group, first=first):
            c = column(group, i)
            pltpu.make_async_copy(tiles_ref.at[c, :, mine], t0.at[first + i], tl.at[group]).start()
            return carry

        lax.fori_loop(0, count, load, 0)

    def fetch(src, dst, sem):
        copy = pltpu.make_async_copy(src, dst, sem)
        copy.start()
        return copy

    get_g = fetch(g_any, g_ref, ins.at[0])
    get_x = [fetch(x_any, xg.at[axis, 3], ins.at[1 + axis]) for axis in (X, Y, Z)]
    get_w = fetch(w_any, w_ref, ins.at[4])

    sent = []

    def finish():
        for region, sem in sent:
            wait(region, sem)

    barrier = pltpu.get_barrier_semaphore()
    pl.semaphore_signal(barrier, inc=1, device_id=partner, device_id_type=MESH)
    for axis in (X, Y, Z):
        for step in (1, 2, 3):
            pl.semaphore_signal(barrier, inc=1, device_id=beside(axis, step), device_id_type=MESH)
    for c in range(32):
        spot = rows_ref[0, 0, c] * 2 + cols_ref[0, 0, c]
        used = jnp.where(counts_ref[0, 0, c] > 0, spot, -1)
        code0[c : c + 1, :] = jnp.full((1, 128), used, jnp.int32).astype(F32)
    get_g.wait()
    gt[...] = g_ref[...].T
    for get in get_x:
        get.wait()
    pl.semaphore_wait(barrier, 10)

    remote(code0, code1, cs, cr, partner)
    sent.append((code0, cs))
    for group, (first, count) in enumerate(GROUPS):

        def swap(i, carry, group=group, first=first):
            c = column(group, i)
            remote(tiles_ref.at[c, :, other], t1.at[first + i], ts.at[group], tr.at[group], partner)
            return carry

        lax.fori_loop(0, count, swap, 0)
        sent.append((t1.at[first : first + count], ts.at[group]))
        if group == 0:
            for axis in (X, Y, Z):
                for step in (2, 1, 3):
                    remote(xg.at[axis, 3], xg.at[axis, step - 1], gs.at[axis], gr.at[axis], beside(axis, step))
                sent.append((xg.at[axis, 0:3], gs.at[axis]))

    wait(code1, cr)

    def send1(part, at1, at2, at3):
        axis = ORDERS[part][0]
        opposite = (at1 // 2) * (1 - at1 % 2)
        way = opposite * (at3 // 2) + (1 - opposite) * (at1 // 2)
        plain = (at1 % 2) * ((at1 // 2 + at3 // 2) % 2)
        block = send[part].at[at1, at2, at3]
        to = beside(axis, 1 + 2 * way)

        @pl.when(opposite == 1)
        def _():
            remote(block, ra[part].at[way, at2, at3 % 2], s1.at[part, at1], ras.at[part, way, at2], to)

        @pl.when(plain == 1)
        def _():
            remote(block, rb[part].at[way, at2, at3], s1.at[part, at1], rbs.at[part, way, at2], to)

    def products(group):
        first, count = GROUPS[group]
        wait(t0.at[first : first + count], tl.at[group])
        wait(t1.at[first : first + count], tr.at[group])

        def one(i, carry):
            dx, dy, dl = place(group, i)
            c = column(group, i)
            near = ((pos[2] + dl) % 4) // 2
            own, theirs = t0[first + i], t1[first + i]
            code_own = code0[pl.ds(c, 1), :]
            code_theirs = code1[pl.ds(c, 1), :]
            lines = []
            for row in range(2):
                line = []
                for col in (near, 1 - near):
                    key = (row * 2 + col).astype(F32)
                    keep_own = jnp.where(code_own == key, 1.0, 0.0).astype(BF16)
                    keep_theirs = jnp.where(code_theirs == key, 1.0, 0.0).astype(BF16)
                    line.append(own * keep_own + theirs * keep_theirs)
                lines.append(jnp.concatenate(line, axis=1))
            dense = jnp.concatenate(lines, axis=0)
            made = jnp.dot(gt[...], dense, preferred_element_type=F32)
            for part in range(3):
                rows = slice(FIRST[part], FIRST[part] + ROWS[part])
                for side in range(2):
                    block = made[rows, side * 128 : (side + 1) * 128]
                    rel = (dx, dy, dl + 2 * side)
                    at = tuple(rel[axis] for axis in ORDERS[part])
                    full[part][at] = block
                    send[part][at] = block.astype(BF16)
            for part in range(3):
                for side in range(2):
                    rel = (dx, dy, dl + 2 * side)
                    send1(part, *(rel[axis] for axis in ORDERS[part]))
            return carry

        lax.fori_loop(0, count, one, 0)

    def merge1(part, t):
        axis = ORDERS[part][0]
        for way, at1, low in ((0, 1, 0), (1, 3, 2)):
            wait(ra[part].at[way, t], ras.at[part, way, t])
            for b in range(2):
                send[part][at1, t, low + b] = (full[part][at1, t, low + b] + ra[part][way, t, b].astype(F32)).astype(BF16)
            pair = slice(low, low + 2)
            remote(
                send[part].at[at1, t, pair],
                rb[part].at[way, t, pair],
                s1.at[part, at1],
                rbs.at[part, way, t],
                beside(axis, 1 + 2 * way),
            )

    def sum1(part, t):
        wait(rb[part].at[0, t], rbs.at[part, 0, t])
        wait(rb[part].at[1, t], rbs.at[part, 1, t])

        def add(b, carry):
            total = full[part][0, t, b] + rb[part][0, t, b].astype(F32) + rb[part][1, t, b].astype(F32)
            full[part][0, t, b] = total
            send[part][0, t, b] = total.astype(BF16)
            return carry

        lax.fori_loop(0, 4, add, 0)

    def step2(part, t):
        axis = ORDERS[part][1]
        sum1(part, t)
        if t > 0:
            remote(send[part].at[0, t], rc[part].at[t - 1], s2.at[part, t - 1], r2.at[part, t - 1], beside(axis, t))

    products(0)
    products(1)
    products(2)
    merge1(1, 2)
    products(3)
    merge1(2, 2)
    merge1(0, 2)
    products(4)
    for t in (1, 3):
        for part in (1, 2, 0):
            merge1(part, t)
    for part in (1, 2, 0):
        step2(part, 2)
        merge1(part, 0)
    for t in (1, 3, 0):
        for part in (1, 2, 0):
            step2(part, t)
    for part in range(3):
        for at1 in (1, 2, 3):
            sent.append((send[part].at[at1], s1.at[part, at1]))
        for t in (1, 2, 3):
            sent.append((send[part].at[0, t], s2.at[part, t - 1]))

    def split(value):
        high = value.astype(BF16)
        return high, (value - high.astype(F32)).astype(BF16)

    for part in (1, 2, 0):
        axis = ORDERS[part][2]
        for t in range(3):
            wait(rc[part].at[t], r2.at[part, t])
        for b in (2, 1, 3, 0):
            near, far, back = (rc[part][t, b].astype(F32) for t in range(3))
            full[part][0, 0, b] = (full[part][0, 0, b] + near) + (far + back)
            if b > 0:
                remote(full[part].at[0, 0, b], rd[part].at[b - 1], s3.at[part, b - 1], r3.at[part, b - 1], beside(axis, b))
        wait(xg.at[axis, 0:3], gr.at[axis])
        high, low = split(jnp.concatenate([full[part][0, 0, b] for b in (3, 2, 1, 0)], axis=1))
        owners = xg[axis].reshape(512, 512)
        gw[FIRST[part] : FIRST[part] + ROWS[part]] = jnp.dot(high, owners, preferred_element_type=F32) + jnp.dot(
            low, owners, preferred_element_type=F32
        )

    kept = pl.ds(pl.multiple_of(core * 256, 256), 256)
    given = pl.ds(pl.multiple_of((1 - core) * 256, 256), 256)
    remote(gw.at[given], gwr, es, er, partner)
    sent.append((gwr, es))
    wait(gwr, er)
    half[...] = gw[kept, :] + gwr[...]

    for part in range(3):
        axis, size = ORDERS[part][0], QUARTER[part]
        for step in (2, 1, 3):
            quarter = pl.ds(pl.multiple_of(QFIRST[part] + ((pos[axis] + step) % 4) * size, 8), size)
            remote(half.at[quarter], x1[part].at[pos[axis]], xs.at[0, part], xr.at[0, part], beside(axis, step))
        x1[part][pos[axis]] = half[pl.ds(pl.multiple_of(QFIRST[part] + pos[axis] * size, 8), size), :]
        sent.append((x1[part].at[0:3], xs.at[0, part]))
    for part in (1, 2, 0):
        for b in range(3):
            wait(rd[part].at[b], r3.at[part, b])
            sent.append((rd[part].at[b], s3.at[part, b]))
        rows = slice(FIRST[part], FIRST[part] + ROWS[part])
        tot[rows] = (full[part][0, 0, 0] + rd[part][0]) + (rd[part][1] + rd[part][2])
    high, low = split(tot[...].T)
    get_w.wait()
    last = (((1,), (1,)), ((), ()))
    gf[...] = lax.dot_general(high, w_ref[...], last, preferred_element_type=F32) + lax.dot_general(
        low, w_ref[...], last, preferred_element_type=F32
    )
    for part in range(3):
        axis = ORDERS[part][1]
        wait(x1[part].at[0:3], xr.at[0, part])
        x1[part][0] = (x1[part][0] + x1[part][1]) + (x1[part][2] + x1[part][3])
        for step in (2, 1, 3):
            lanes = pl.ds(pl.multiple_of(((pos[axis] + step) % 4) * 128, 128), 128)
            remote(x1[part].at[0, :, lanes], x2[part].at[pos[axis]], xs.at[1, part], xr.at[1, part], beside(axis, step))
        x2[part][pos[axis]] = x1[part][0, :, pl.ds(pl.multiple_of(pos[axis] * 128, 128), 128)]
        sent.append((x2[part].at[0:3], xs.at[1, part]))
    for part in range(3):
        axis = ORDERS[part][2]
        wait(x2[part].at[0:3], xr.at[1, part])
        x3[part][pos[axis]] = (x2[part][0] + x2[part][1]) + (x2[part][2] + x2[part][3])
        for step in (2, 1, 3):
            here = x3[part].at[pos[axis]]
            remote(here, here, xs.at[2, part], xr.at[2, part], beside(axis, step))
        sent.append((x3[part].at[0:3], xs.at[2, part]))
    for part in range(3):
        axis, size = ORDERS[part][1], QUARTER[part]
        wait(x3[part].at[0:3], xr.at[2, part])
        lanes = pl.ds(pl.multiple_of(pos[axis] * 128, 128), 128)
        rows = pl.ds(pl.multiple_of(core * 256 + QFIRST[part] + pos[ORDERS[part][0]] * size, 8), size)
        gw_out[rows, lanes] = (x3[part][0] + x3[part][1]) + (x3[part][2] + x3[part][3])
        here = gw_out.at[rows, lanes]
        for step in (2, 1, 3):
            remote(here, here, xs.at[3, part], xr.at[3, part], beside(axis, step))
        sent.append((x3[part].at[0:3], xs.at[3, part]))

    for part in range(3):
        axis, size = ORDERS[part][0], QUARTER[part]
        wait(x3[part].at[0:3], xr.at[3, part])
        rows = pl.ds(pl.multiple_of(core * 256 + QFIRST[part] + pos[axis] * size, 8), size)
        here = gw_out.at[rows]
        for step in (2, 1, 3):
            remote(here, here, xs.at[4, part], xr.at[4, part], beside(axis, step))
        remote(here, here, fs.at[0, part], fr.at[0, part], partner)
        sent.append((half.at[0 : 3 * size], xs.at[4, part]))
        sent.append((half.at[0:size], fs.at[0, part]))
    for part in range(3):
        axis, size = ORDERS[part][0], QUARTER[part]
        wait(half.at[0 : 3 * size], xr.at[4, part])
        for step in (1, 2, 3):
            first = core * 256 + QFIRST[part] + ((pos[axis] + step) % 4) * size
            here = gw_out.at[pl.ds(pl.multiple_of(first, 8), size)]
            remote(here, here, fs.at[1, part], fr.at[1, part], partner)
        sent.append((half.at[0 : 3 * size], fs.at[1, part]))
    for part in range(3):
        size = QUARTER[part]
        wait(half.at[0:size], fr.at[0, part])
        wait(half.at[0 : 3 * size], fr.at[1, part])
    finish()


def body(tile_values, tile_rows, tile_cols, tile_counts, grad_out, features, weight):
    tiles = tile_values[0, 0, :, 0]
    anywhere = pl.BlockSpec(memory_space=pl.ANY)
    smem = pl.BlockSpec(memory_space=pltpu.SMEM)

    def per_part(*shape, dtype, rows=ROWS, lanes=128):
        return [pltpu.VMEM((*shape, r, lanes), dtype) for r in rows]

    dma = pltpu.SemaphoreType.DMA
    scratch = [
        pltpu.VMEM((32, 256, 128), BF16),
        pltpu.VMEM((32, 256, 128), BF16),
        pltpu.VMEM((32, 128), F32),
        pltpu.VMEM((32, 128), F32),
        pltpu.VMEM((512, 512), BF16),
        pltpu.VMEM((512, 512), BF16),
        pltpu.VMEM((512, 512), BF16),
        pltpu.VMEM((3, 4, 128, 512), BF16),
        *per_part(4, 4, 4, dtype=BF16),
        *per_part(4, 4, 4, dtype=F32),
        *per_part(2, 4, 2, dtype=BF16),
        *per_part(2, 4, 4, dtype=BF16),
        *per_part(3, 4, dtype=BF16),
        *per_part(3, dtype=F32),
        pltpu.VMEM((512, 128), F32),
        pltpu.VMEM((512, 512), F32),
        pltpu.VMEM((256, 512), F32),
        pltpu.VMEM((256, 512), F32),
    ]
    for lanes in (512, 128, 128):
        scratch += per_part(4, dtype=F32, rows=QUARTER, lanes=lanes)
    scratch += [
        dma((5,)),
        dma((3,)),
        dma((3,)),
        dma((5,)),
        dma((5,)),
        dma((5,)),
        dma,
        dma,
        dma((3, 4)),
        dma((3, 2, 4)),
        dma((3, 2, 4)),
        dma((3, 3)),
        dma((3, 3)),
        dma((3, 3)),
        dma((3, 3)),
        dma,
        dma,
        dma((5, 3)),
        dma((5, 3)),
        dma((2, 3)),
        dma((2, 3)),
    ]
    vmem = pl.BlockSpec(memory_space=pltpu.VMEM)
    grad_features, turned = pl.pallas_call(
        kernel,
        out_shape=(pltpu.VMEM((128, 512), F32), pltpu.VMEM((512, 512), F32)),
        in_specs=[smem, smem, smem, anywhere, anywhere, anywhere, anywhere],
        out_specs=(vmem, vmem),
        scratch_shapes=scratch,
        compiler_params=pltpu.CompilerParams(
            collective_id=0, has_side_effects=True, vmem_limit_bytes=56 * 1024 * 1024
        ),
    )(tile_rows[..., 0], tile_cols[..., 0], tile_counts, tiles, grad_out, features, weight)
    return grad_features, turned.T


def solution(mesh):
    placed = (
        P("blk", "rep", None, None, None, None),
        P("blk", "rep", None, None),
        P("blk", "rep", None, None),
        P("blk", "rep", None),
        P("blk", None),
        P(("blk", "rep"), None),
        P(),
    )
    return jax.shard_map(
        body, mesh=mesh, in_specs=placed, out_specs=(P(("blk", "rep"), None), P()), check_vma=False
    )
```

```python
import functools

import jax
import jax.numpy as jnp
from jax import lax
from jax.experimental import pallas as pl
from jax.experimental.pallas import tpu as pltpu
from jax.sharding import PartitionSpec as P

MESH = pl.DeviceIdType.MESH
F32 = jnp.float32
BF16 = jnp.bfloat16

ROWS = (176, 176, 160)
FIRST = (0, 176, 352)
X, Y, Z = 0, 1, 2
ORDERS = ((X, Z, Y), (Y, X, Z), (Z, Y, X))
QUARTER = (48, 48, 32)
QFIRST = (0, 192, 384)
PLACES = (2, 1, 3, 0)


def kernel(rows_ref, cols_ref, counts_ref, tiles_ref, g_any, x_any, w_any, gf, gw_out, *scratch):
    (t0, t1, code0, code1, g_ref, w_ref, gt, xg, *rest) = scratch
    send = rest[0:3]
    full = rest[3:6]
    ra, rb, rc, rd = rest[6:9], rest[9:12], rest[12:15], rest[15:18]
    tot, gw, gwr, half = rest[18:22]
    x1, x2, x3 = rest[22:25], rest[25:28], rest[28:31]
    (ins, gs, gr, tl, ts, tr, cs, cr, s1, ras, rbs, rps, s2, r2, s3, r3, es, er, xs, xr, fs, fr) = rest[31:]

    blk = lax.axis_index("blk")
    rep = lax.axis_index("rep")
    core = rep % 2
    pos = (blk // 8, (blk // 2) % 4, (rep // 2) * 2 + blk % 2)

    def device(where, which):
        return (where[0] * 8 + where[1] * 2 + where[2] % 2, (where[2] // 2) * 2 + which)

    def beside(axis, step):
        where = list(pos)
        where[axis] = (pos[axis] + step) % 4
        return device(where, core)

    partner = device(pos, 1 - core)

    def remote(src, dst, ssem, rsem, to):
        pltpu.make_async_remote_copy(
            src_ref=src, dst_ref=dst, send_sem=ssem, recv_sem=rsem, device_id=to, device_id_type=MESH
        ).start()

    def wait(ref, sem):
        pltpu.make_async_copy(ref, ref, sem).wait()

    mine = pl.ds(pl.multiple_of(core * 128, 128), 128)
    other = pl.ds(pl.multiple_of((1 - core) * 128, 128), 128)

    def columns(n):
        return pl.ds(((pos[0] + PLACES[n]) % 4) * 8, 8)

    for n in range(4):
        pltpu.make_async_copy(tiles_ref.at[columns(n), :, mine], t0.at[8 * n : 8 * n + 8], tl.at[n]).start()

    def fetch(src, dst, sem):
        copy = pltpu.make_async_copy(src, dst, sem)
        copy.start()
        return copy

    get_g = fetch(g_any, g_ref, ins.at[0])
    get_x = [fetch(x_any, xg.at[axis, 3], ins.at[1 + axis]) for axis in (X, Y, Z)]
    get_w = fetch(w_any, w_ref, ins.at[4])

    sent = []

    def finish():
        for region, sem in sent:
            wait(region, sem)

    barrier = pltpu.get_barrier_semaphore()
    pl.semaphore_signal(barrier, inc=1, device_id=partner, device_id_type=MESH)
    for axis in (X, Y, Z):
        for step in (1, 2, 3):
            pl.semaphore_signal(barrier, inc=1, device_id=beside(axis, step), device_id_type=MESH)
    for c in range(32):
        spot = rows_ref[0, 0, c] * 2 + cols_ref[0, 0, c]
        used = jnp.where(counts_ref[0, 0, c] > 0, spot, -1)
        code0[c : c + 1, :] = jnp.full((1, 128), used, jnp.int32).astype(F32)
    get_g.wait()
    gt[...] = g_ref[...].T
    for get in get_x:
        get.wait()
    pl.semaphore_wait(barrier, 10)

    remote(code0, code1, cs, cr, partner)
    sent.append((code0, cs))
    for n in range(4):
        slots = slice(8 * n, 8 * n + 8)
        remote(tiles_ref.at[columns(n), :, other], t1.at[slots], ts.at[n], tr.at[n], partner)
        sent.append((t1.at[slots], ts.at[n]))
    for axis in (X, Y, Z):
        for step in (2, 1, 3):
            remote(xg.at[axis, 3], xg.at[axis, step - 1], gs.at[axis], gr.at[axis], beside(axis, step))
        sent.append((xg.at[axis, 0:3], gs.at[axis]))

    wait(code1, cr)

    def send_x(dx, dy):
        if dx == 2:
            way = dy // 2
            to = beside(X, 1 + 2 * way)
            remote(send[0].at[2, :, dy], ra[0].at[way, :, dy % 2], s1.at[0, 2], ras.at[0, way, 0], to)
        if dx % 2 == 1:
            way = dx // 2

            @pl.when(dy // 2 != way)
            def _():
                block = send[0].at[dx, :, dy]
                remote(block, rb[0].at[way, :, dy], s1.at[0, dx], rps.at[way], beside(X, dx))

    def send_y(dx, dy):
        @pl.when(dy == 2)
        def _():
            for way in range(2):
                pair = slice(2 * way, 2 * way + 2)
                to = beside(Y, 1 + 2 * way)
                remote(send[1].at[2, dx, pair], ra[1].at[way, dx], s1.at[1, 2], ras.at[1, way, dx], to)

        @pl.when(dy % 2 == 1)
        def _():
            way = dy // 2
            pair = pl.ds(2 - 2 * way, 2)
            block = send[1].at[dy, dx, pair]
            remote(block, rb[1].at[way, dx, pair], s1.at[1, dy], rbs.at[1, way, dx], beside(Y, 1 + 2 * way))

    def send_z(dx, dy):
        way = dx // 2
        to = beside(Z, 1 + 2 * way)
        remote(send[2].at[2, dy, dx], ra[2].at[way, dy, dx % 2], s1.at[2, 2], ras.at[2, way, dy], to)
        way = 1 - way
        at1 = 1 + 2 * way
        remote(send[2].at[at1, dy, dx], rb[2].at[way, dy, dx], s1.at[2, at1], rbs.at[2, way, dy], beside(Z, at1))

    def products(n):
        dx = PLACES[n]
        wait(t0.at[8 * n : 8 * n + 8], tl.at[n])
        wait(t1.at[8 * n : 8 * n + 8], tr.at[n])

        def one(i, carry):
            dy = (i + 2) % 4
            for dl in range(2):
                offset = ((pos[1] + dy) % 4) * 2 + (pos[2] + dl) % 2
                c = ((pos[0] + dx) % 4) * 8 + offset
                near = ((pos[2] + dl) % 4) // 2
                own, theirs = t0[8 * n + offset], t1[8 * n + offset]
                code_own = code0[pl.ds(c, 1), :]
                code_theirs = code1[pl.ds(c, 1), :]
                lines = []
                for row in range(2):
                    line = []
                    for col in (near, 1 - near):
                        key = (row * 2 + col).astype(F32)
                        keep_own = jnp.where(code_own == key, 1.0, 0.0).astype(BF16)
                        keep_theirs = jnp.where(code_theirs == key, 1.0, 0.0).astype(BF16)
                        line.append(own * keep_own + theirs * keep_theirs)
                    lines.append(jnp.concatenate(line, axis=1))
                dense = jnp.concatenate(lines, axis=0)
                made = jnp.dot(gt[...], dense, preferred_element_type=F32)
                for part in range(3):
                    rows = slice(FIRST[part], FIRST[part] + ROWS[part])
                    for side in range(2):
                        block = made[rows, side * 128 : (side + 1) * 128]
                        rel = (dx, dy, dl + 2 * side)
                        at = tuple(rel[axis] for axis in ORDERS[part])
                        fixed = at[0] if isinstance(at[0], int) else 1
                        if fixed != 2:
                            full[part][at] = block
                        if fixed != 0:
                            send[part][at] = block.astype(BF16)
            send_x(dx, dy)
            send_y(dx, dy)
            send_z(dx, dy)
            return carry

        lax.fori_loop(0, 4, one, 0)

    def merge1(part, t):
        axis = ORDERS[part][0]
        for way, at1, low in ((0, 1, 0), (1, 3, 2)):
            if part > 0:
                wait(ra[part].at[way, t], ras.at[part, way, t])
            elif t == 2:
                wait(ra[part].at[way], ras.at[part, way, 0])
            for b in range(2):
                send[part][at1, t, low + b] = (full[part][at1, t, low + b] + ra[part][way, t, b].astype(F32)).astype(BF16)
            pair = slice(low, low + 2)
            remote(
                send[part].at[at1, t, pair],
                rb[part].at[way, t, pair],
                s1.at[part, at1],
                rbs.at[part, way, t],
                beside(axis, 1 + 2 * way),
            )

    def sum1(part, t):
        for way in range(2):
            if part > 0:
                wait(rb[part].at[way, t], rbs.at[part, way, t])
            else:
                wait(rb[part].at[way, t, 0:2], rbs.at[part, way, t])
                if t == 2:
                    wait(rb[part].at[way, :, 0:2], rps.at[way])

        def add(b, carry):
            total = full[part][0, t, b] + rb[part][0, t, b].astype(F32) + rb[part][1, t, b].astype(F32)
            full[part][0, t, b] = total
            send[part][0, t, b] = total.astype(BF16)
            return carry

        lax.fori_loop(0, 4, add, 0)

    def step2(part, t):
        axis = ORDERS[part][1]
        sum1(part, t)
        if t > 0:
            remote(send[part].at[0, t], rc[part].at[t - 1], s2.at[part, t - 1], r2.at[part, t - 1], beside(axis, t))

    products(0)
    products(1)
    merge1(1, 2)
    products(2)
    merge1(0, 2)
    merge1(1, 1)
    products(3)
    for part, t in ((2, 2), (0, 1), (1, 3), (2, 1), (0, 3), (2, 3)):
        merge1(part, t)
    for part in (1, 0, 2):
        step2(part, 2)
        merge1(part, 0)
    for t in (1, 3, 0):
        for part in (1, 2, 0):
            step2(part, t)
    for part in range(3):
        for at1 in (1, 2, 3):
            sent.append((send[part].at[at1], s1.at[part, at1]))
        for t in (1, 2, 3):
            sent.append((send[part].at[0, t], s2.at[part, t - 1]))

    def split(value):
        high = value.astype(BF16)
        return high, (value - high.astype(F32)).astype(BF16)

    kept = pl.ds(pl.multiple_of(core * 256, 256), 256)
    given = pl.ds(pl.multiple_of((1 - core) * 256, 256), 256)
    for part in range(3):
        axis = ORDERS[part][2]
        for t in range(3):
            wait(rc[part].at[t], r2.at[part, t])
        for b in range(4):
            near, far, back = (rc[part][t, b].astype(F32) for t in range(3))
            full[part][0, 0, b] = (full[part][0, 0, b] + near) + (far + back)
        wait(xg.at[axis, 0:3], gr.at[axis])
        high, low = split(jnp.concatenate([full[part][0, 0, b] for b in (3, 2, 1, 0)], axis=1))
        owners = xg[axis].reshape(512, 512)
        rows = slice(FIRST[part], FIRST[part] + ROWS[part])
        gw[rows] = jnp.dot(high, owners, preferred_element_type=F32) + jnp.dot(low, owners, preferred_element_type=F32)
        remote(gw.at[rows, given], gwr.at[rows], es.at[part], er.at[part], partner)
        sent.append((gwr.at[rows], es.at[part]))

    def stage3(part):
        axis = ORDERS[part][2]
        for b in (2, 1, 3):
            remote(full[part].at[0, 0, b], rd[part].at[b - 1], s3.at[part, b - 1], r3.at[part, b - 1], beside(axis, b))
            sent.append((rd[part].at[b - 1], s3.at[part, b - 1]))

    def merge_cores(part):
        rows = slice(FIRST[part], FIRST[part] + ROWS[part])
        wait(gwr.at[rows], er.at[part])
        half[rows] = gw[rows, kept] + gwr[rows]

    def scatter(part):
        axis, size = ORDERS[part][0], QUARTER[part]
        for step in (2, 1, 3):
            quarter = pl.ds(pl.multiple_of(QFIRST[part] + ((pos[axis] + step) % 4) * size, 8), size)
            remote(half.at[quarter], x1[part].at[pos[axis]], xs.at[0, part], xr.at[0, part], beside(axis, step))
        x1[part][pos[axis]] = half[pl.ds(pl.multiple_of(QFIRST[part] + pos[axis] * size, 8), size), :]
        sent.append((x1[part].at[0:3], xs.at[0, part]))

    merge_cores(0)
    merge_cores(1)
    scatter(0)
    merge_cores(2)
    scatter(1)
    scatter(2)
    stage3(0)
    for stage, (took, gave) in enumerate(((x1, x2), (x2, x3))):
        for part in range(3):
            axis = ORDERS[part][stage + 1]
            wait(took[part].at[0:3], xr.at[stage, part])
            gave[part][pos[axis]] = (took[part][0] + took[part][1]) + (took[part][2] + took[part][3])
            here = gave[part].at[pos[axis]]
            for step in (2, 1, 3):
                remote(here, here, xs.at[stage + 1, part], xr.at[stage + 1, part], beside(axis, step))
            sent.append((gave[part].at[0:3], xs.at[stage + 1, part]))
        stage3(stage + 1)
    for part in range(3):
        axis, size = ORDERS[part][0], QUARTER[part]
        wait(x3[part].at[0:3], xr.at[2, part])
        rows = pl.ds(pl.multiple_of(QFIRST[part] + pos[axis] * size, 8), size)
        gw_out[rows, kept] = (x3[part][0] + x3[part][1]) + (x3[part][2] + x3[part][3])
        here = gw_out.at[rows, kept]
        for step in (2, 1, 3):
            remote(here, here, xs.at[3, part], xr.at[3, part], beside(axis, step))
        remote(here, here, fs.at[0, part], fr.at[0, part], partner)
        sent.append((x3[part].at[0:3], xs.at[3, part]))
        sent.append((x3[part].at[0], fs.at[0, part]))

    for part in range(3):
        for b in range(3):
            wait(rd[part].at[b], r3.at[part, b])
        rows = slice(FIRST[part], FIRST[part] + ROWS[part])
        tot[rows] = (full[part][0, 0, 0] + rd[part][0]) + (rd[part][1] + rd[part][2])
    high, low = split(tot[...].T)
    get_w.wait()
    last = (((1,), (1,)), ((), ()))
    gf[...] = lax.dot_general(high, w_ref[...], last, preferred_element_type=F32) + lax.dot_general(
        low, w_ref[...], last, preferred_element_type=F32
    )

    for part in range(3):
        axis, size = ORDERS[part][0], QUARTER[part]
        wait(x3[part].at[0:3], xr.at[3, part])
        for step in (1, 2, 3):
            rows = pl.ds(pl.multiple_of(QFIRST[part] + ((pos[axis] + step) % 4) * size, 8), size)
            here = gw_out.at[rows, kept]
            remote(here, here, fs.at[1, part], fr.at[1, part], partner)
        sent.append((x3[part].at[0:3], fs.at[1, part]))
    for part in range(3):
        wait(x3[part].at[0], fr.at[0, part])
        wait(x3[part].at[0:3], fr.at[1, part])
    finish()


def body(tile_values, tile_rows, tile_cols, tile_counts, grad_out, features, weight):
    tiles = tile_values[0, 0, :, 0]
    anywhere = pl.BlockSpec(memory_space=pl.ANY)
    smem = pl.BlockSpec(memory_space=pltpu.SMEM)

    def per_part(*shape, dtype, rows=ROWS, lanes=128):
        return [pltpu.VMEM((*shape, r, lanes), dtype) for r in rows]

    dma = pltpu.SemaphoreType.DMA
    scratch = [
        pltpu.VMEM((32, 256, 128), BF16),
        pltpu.VMEM((32, 256, 128), BF16),
        pltpu.VMEM((32, 128), F32),
        pltpu.VMEM((32, 128), F32),
        pltpu.VMEM((512, 512), BF16),
        pltpu.VMEM((512, 512), BF16),
        pltpu.VMEM((512, 512), BF16),
        pltpu.VMEM((3, 4, 128, 512), BF16),
        *per_part(4, 4, 4, dtype=BF16),
        *per_part(4, 4, 4, dtype=F32),
        *per_part(2, 4, 2, dtype=BF16),
        *per_part(2, 4, 4, dtype=BF16),
        *per_part(3, 4, dtype=BF16),
        *per_part(3, dtype=F32),
        pltpu.VMEM((512, 128), F32),
        pltpu.VMEM((512, 512), F32),
        pltpu.VMEM((512, 256), F32),
        pltpu.VMEM((512, 256), F32),
    ]
    for _ in range(3):
        scratch += per_part(4, dtype=F32, rows=QUARTER, lanes=256)
    scratch += [
        dma((5,)),
        dma((3,)),
        dma((3,)),
        dma((4,)),
        dma((4,)),
        dma((4,)),
        dma,
        dma,
        dma((3, 4)),
        dma((3, 2, 4)),
        dma((3, 2, 4)),
        dma((2,)),
        dma((3, 3)),
        dma((3, 3)),
        dma((3, 3)),
        dma((3, 3)),
        dma((3,)),
        dma((3,)),
        dma((4, 3)),
        dma((4, 3)),
        dma((2, 3)),
        dma((2, 3)),
    ]
    vmem = pl.BlockSpec(memory_space=pltpu.VMEM)
    grad_features, turned = pl.pallas_call(
        kernel,
        out_shape=(pltpu.VMEM((128, 512), F32), pltpu.VMEM((512, 512), F32)),
        in_specs=[smem, smem, smem, anywhere, anywhere, anywhere, anywhere],
        out_specs=(vmem, vmem),
        scratch_shapes=scratch,
        compiler_params=pltpu.CompilerParams(
            collective_id=0, has_side_effects=True, vmem_limit_bytes=56 * 1024 * 1024
        ),
    )(tile_rows[..., 0], tile_cols[..., 0], tile_counts, tiles, grad_out, features, weight)
    return grad_features, turned.T


def solution(mesh):
    placed = (
        P("blk", "rep", None, None, None, None),
        P("blk", "rep", None, None),
        P("blk", "rep", None, None),
        P("blk", "rep", None),
        P("blk", None),
        P(("blk", "rep"), None),
        P(),
    )
    return jax.shard_map(
        body, mesh=mesh, in_specs=placed, out_specs=(P(("blk", "rep"), None), P()), check_vma=False
    )
```

```python
import functools

import jax
import jax.numpy as jnp
from jax import lax
from jax.experimental import pallas as pl
from jax.experimental.pallas import tpu as pltpu
from jax.sharding import PartitionSpec as P

MESH = pl.DeviceIdType.MESH
F32 = jnp.float32
BF16 = jnp.bfloat16

ROWS = (176, 176, 160)
FIRST = (0, 176, 352)
X, Y, Z = 0, 1, 2
ORDERS = ((X, Z, Y), (Y, X, Z), (Z, Y, X))
QUARTER = (48, 48, 32)
QFIRST = (0, 192, 384)
PLACES = (2, 1, 3, 0)


def kernel(rows_ref, cols_ref, counts_ref, tiles_ref, g_any, x_any, w_any, gf, gw_out, *scratch):
    (t0, t1, code0, code1, g_ref, w_ref, gt, xg, *rest) = scratch
    send = rest[0:3]
    full = rest[3:6]
    ra, rb, r2a, rc, rd = rest[6:9], rest[9:12], rest[12:15], rest[15:18], rest[18:21]
    tot, gw, gwr, half = rest[21:25]
    x1, x2, x3 = rest[25:28], rest[28:31], rest[31:34]
    (ins, gs, gr, tl, ts, tr, cs, cr, s1, ras, rbs, rps, s2, r2, s3, r3, es, er, xs, xr, fs, fr) = rest[34:]

    blk = lax.axis_index("blk")
    rep = lax.axis_index("rep")
    core = rep % 2
    pos = (blk // 8, (blk // 2) % 4, (rep // 2) * 2 + blk % 2)

    def device(where, which):
        return (where[0] * 8 + where[1] * 2 + where[2] % 2, (where[2] // 2) * 2 + which)

    def beside(axis, step):
        where = list(pos)
        where[axis] = (pos[axis] + step) % 4
        return device(where, core)

    partner = device(pos, 1 - core)

    def remote(src, dst, ssem, rsem, to):
        pltpu.make_async_remote_copy(
            src_ref=src, dst_ref=dst, send_sem=ssem, recv_sem=rsem, device_id=to, device_id_type=MESH
        ).start()

    def wait(ref, sem):
        pltpu.make_async_copy(ref, ref, sem).wait()

    mine = pl.ds(pl.multiple_of(core * 128, 128), 128)
    other = pl.ds(pl.multiple_of((1 - core) * 128, 128), 128)

    barrier = pltpu.get_barrier_semaphore()
    for axis in (X, Y, Z):
        for step in (2, 1, 3):
            pl.semaphore_signal(barrier, inc=1, device_id=beside(axis, step), device_id_type=MESH)
    pl.semaphore_signal(barrier, inc=1, device_id=partner, device_id_type=MESH)

    def columns(n):
        return pl.ds(((pos[0] + PLACES[n]) % 4) * 8, 8)

    def fetch(src, dst, sem):
        copy = pltpu.make_async_copy(src, dst, sem)
        copy.start()
        return copy

    get_g = fetch(g_any, g_ref, ins.at[0])
    for n in range(4):
        fetch(tiles_ref.at[columns(n), :, mine], t0.at[8 * n : 8 * n + 8], tl.at[n])
    get_x = [fetch(x_any, xg.at[axis, 3], ins.at[1 + axis]) for axis in (X, Y, Z)]
    get_w = fetch(w_any, w_ref, ins.at[4])

    sent = []

    def finish():
        for region, sem in sent:
            wait(region, sem)

    for c in range(32):
        spot = rows_ref[0, 0, c] * 2 + cols_ref[0, 0, c]
        used = jnp.where(counts_ref[0, 0, c] > 0, spot, -1)
        code0[c : c + 1, :] = jnp.full((1, 128), used, jnp.int32).astype(F32)
    pl.semaphore_wait(barrier, 10)

    def swap(n):
        slots = slice(8 * n, 8 * n + 8)
        remote(tiles_ref.at[columns(n), :, other], t1.at[slots], ts.at[n], tr.at[n], partner)
        sent.append((t1.at[slots], ts.at[n]))

    remote(code0, code1, cs, cr, partner)
    sent.append((code0, cs))
    swap(0)
    for axis in (X, Y, Z):
        for step in (2, 1, 3):
            remote(x_any, xg.at[axis, step - 1], gs.at[axis], gr.at[axis], beside(axis, step))
        sent.append((xg.at[axis, 0:3], gs.at[axis]))
    for n in range(1, 4):
        swap(n)
    get_g.wait()
    gt[...] = g_ref[...].T
    for get in get_x:
        get.wait()
    wait(code1, cr)

    def send_x(dx, dy):
        if dx == 2:
            way = dy // 2
            to = beside(X, 1 + 2 * way)
            remote(send[0].at[2, :, dy], ra[0].at[way, :, dy % 2], s1.at[0, 2], ras.at[0, way, 0], to)
        if dx % 2 == 1:
            way = dx // 2

            @pl.when(dy // 2 != way)
            def _():
                block = send[0].at[dx, :, dy]
                remote(block, rb[0].at[way, :, dy], s1.at[0, dx], rps.at[way], beside(X, dx))

    def send_y(dx, dy):
        @pl.when(dy == 2)
        def _():
            for way in range(2):
                pair = slice(2 * way, 2 * way + 2)
                to = beside(Y, 1 + 2 * way)
                remote(send[1].at[2, dx, pair], ra[1].at[way, dx], s1.at[1, 2], ras.at[1, way, dx], to)

        @pl.when(dy % 2 == 1)
        def _():
            way = dy // 2
            pair = pl.ds(2 - 2 * way, 2)
            block = send[1].at[dy, dx, pair]
            remote(block, rb[1].at[way, dx, pair], s1.at[1, dy], rbs.at[1, way, dx], beside(Y, 1 + 2 * way))

    def send_z(dx, dy):
        way = dx // 2
        to = beside(Z, 1 + 2 * way)
        remote(send[2].at[2, dy, dx], ra[2].at[way, dy, dx % 2], s1.at[2, 2], ras.at[2, way, dy], to)
        way = 1 - way
        at1 = 1 + 2 * way
        remote(send[2].at[at1, dy, dx], rb[2].at[way, dy, dx], s1.at[2, at1], rbs.at[2, way, dy], beside(Z, at1))

    def products(n):
        dx = PLACES[n]
        wait(t0.at[8 * n : 8 * n + 8], tl.at[n])
        wait(t1.at[8 * n : 8 * n + 8], tr.at[n])

        def one(i, carry):
            dy = (i + 2) % 4
            for dl in range(2):
                offset = ((pos[1] + dy) % 4) * 2 + (pos[2] + dl) % 2
                c = ((pos[0] + dx) % 4) * 8 + offset
                near = ((pos[2] + dl) % 4) // 2
                own, theirs = t0[8 * n + offset], t1[8 * n + offset]
                code_own = code0[pl.ds(c, 1), :]
                code_theirs = code1[pl.ds(c, 1), :]
                lines = []
                for row in range(2):
                    line = []
                    for col in (near, 1 - near):
                        key = (row * 2 + col).astype(F32)
                        keep_own = jnp.where(code_own == key, 1.0, 0.0).astype(BF16)
                        keep_theirs = jnp.where(code_theirs == key, 1.0, 0.0).astype(BF16)
                        line.append(own * keep_own + theirs * keep_theirs)
                    lines.append(jnp.concatenate(line, axis=1))
                dense = jnp.concatenate(lines, axis=0)
                made = jnp.dot(gt[...], dense, preferred_element_type=F32)
                for part in range(3):
                    rows = slice(FIRST[part], FIRST[part] + ROWS[part])
                    for side in range(2):
                        block = made[rows, side * 128 : (side + 1) * 128]
                        rel = (dx, dy, dl + 2 * side)
                        at = tuple(rel[axis] for axis in ORDERS[part])
                        fixed = at[0] if isinstance(at[0], int) else 1
                        if fixed != 2:
                            full[part][at] = block
                        if fixed != 0:
                            send[part][at] = block.astype(BF16)
            send_x(dx, dy)
            send_y(dx, dy)
            send_z(dx, dy)
            return carry

        lax.fori_loop(0, 4, one, 0)

    def merge1(part, t):
        axis = ORDERS[part][0]
        for way, at1, low in ((0, 1, 0), (1, 3, 2)):
            if part > 0:
                wait(ra[part].at[way, t], ras.at[part, way, t])
            elif t == 2:
                wait(ra[part].at[way], ras.at[part, way, 0])
            for b in range(2):
                send[part][at1, t, low + b] = (full[part][at1, t, low + b] + ra[part][way, t, b].astype(F32)).astype(BF16)
            pair = slice(low, low + 2)
            remote(
                send[part].at[at1, t, pair],
                rb[part].at[way, t, pair],
                s1.at[part, at1],
                rbs.at[part, way, t],
                beside(axis, 1 + 2 * way),
            )

    def sum1(part, t):
        for way in range(2):
            if part > 0:
                wait(rb[part].at[way, t], rbs.at[part, way, t])
            else:
                wait(rb[part].at[way, t, 0:2], rbs.at[part, way, t])
                if t == 2:
                    wait(rb[part].at[way, :, 0:2], rps.at[way])

        def add(b, carry):
            total = full[part][0, t, b] + rb[part][0, t, b].astype(F32) + rb[part][1, t, b].astype(F32)
            full[part][0, t, b] = total
            send[part][0, t, b] = total.astype(BF16)
            return carry

        lax.fori_loop(0, 4, add, 0)

    def step2(part, t):
        axis = ORDERS[part][1]
        sum1(part, t)
        if t > 0:
            source = send[part].at[0, t]
        if t == 2:
            for way in range(2):
                pair = source.at[2 * way : 2 * way + 2]
                remote(pair, r2a[part].at[way], s2.at[part, 0], r2.at[part, way], beside(axis, 1 + 2 * way))
        elif t > 0:
            way = t // 2
            pair = slice(2 - 2 * way, 4 - 2 * way)
            remote(source.at[pair], rc[part].at[way, pair], s2.at[part, t], r2.at[part, 2 + way], beside(axis, t))

    def merge2(part):
        axis = ORDERS[part][1]
        for way, t in ((0, 1), (1, 3)):
            wait(r2a[part].at[way], r2.at[part, way])
            for b in range(2):
                at = (0, t, 2 * way + b)
                send[part][at] = (full[part][at] + r2a[part][way, b].astype(F32)).astype(BF16)
            pair = slice(2 * way, 2 * way + 2)
            source = send[part].at[0, t, pair]
            remote(source, rc[part].at[way, pair], s2.at[part, t], r2.at[part, 2 + way], beside(axis, t))

    products(0)
    products(1)
    merge1(1, 2)
    products(2)
    merge1(0, 2)
    merge1(1, 1)
    products(3)
    for part, t in ((2, 2), (0, 1), (1, 3), (2, 1), (0, 3), (2, 3)):
        merge1(part, t)
    for part in (1, 0, 2):
        step2(part, 2)
        merge1(part, 0)
    for t in (1, 3):
        for part in (1, 0, 2):
            step2(part, t)
            if t == 3:
                merge2(part)
    for part in (1, 0, 2):
        step2(part, 0)
    for part in range(3):
        for at1 in (1, 2, 3):
            sent.append((send[part].at[at1], s1.at[part, at1]))
        for t, sem in ((1, 1), (2, 0), (3, 3)):
            sent.append((send[part].at[0, t], s2.at[part, sem]))

    def split(value):
        high = value.astype(BF16)
        return high, (value - high.astype(F32)).astype(BF16)

    kept = pl.ds(pl.multiple_of(core * 256, 256), 256)
    given = pl.ds(pl.multiple_of((1 - core) * 256, 256), 256)
    for part in range(3):
        axis = ORDERS[part][2]
        for way in range(2):
            wait(rc[part].at[way], r2.at[part, 2 + way])
        for b in range(4):
            near, back = (rc[part][way, b].astype(F32) for way in range(2))
            full[part][0, 0, b] = full[part][0, 0, b] + (near + back)
        wait(xg.at[axis, 0:3], gr.at[axis])
        high, low = split(jnp.concatenate([full[part][0, 0, b] for b in (3, 2, 1, 0)], axis=1))
        owners = xg[axis].reshape(512, 512)
        rows = slice(FIRST[part], FIRST[part] + ROWS[part])
        gw[rows] = jnp.dot(high, owners, preferred_element_type=F32) + jnp.dot(low, owners, preferred_element_type=F32)
        remote(gw.at[rows, given], gwr.at[rows], es.at[part], er.at[part], partner)
        sent.append((gwr.at[rows], es.at[part]))

    def stage3(*places):
        for part in range(3):
            axis = ORDERS[part][2]
            for b in places:
                remote(full[part].at[0, 0, b], rd[part].at[b - 1], s3.at[part, b - 1], r3.at[part, b - 1], beside(axis, b))
                sent.append((rd[part].at[b - 1], s3.at[part, b - 1]))

    def merge_cores(part):
        rows = slice(FIRST[part], FIRST[part] + ROWS[part])
        wait(gwr.at[rows], er.at[part])
        half[rows] = gw[rows, kept] + gwr[rows]

    def scatter(part):
        axis, size = ORDERS[part][0], QUARTER[part]
        for step in (2, 1, 3):
            quarter = pl.ds(pl.multiple_of(QFIRST[part] + ((pos[axis] + step) % 4) * size, 8), size)
            remote(half.at[quarter], x1[part].at[pos[axis]], xs.at[0, part], xr.at[0, part], beside(axis, step))
        x1[part][pos[axis]] = half[pl.ds(pl.multiple_of(QFIRST[part] + pos[axis] * size, 8), size), :]
        sent.append((x1[part].at[0:3], xs.at[0, part]))

    merge_cores(0)
    merge_cores(1)
    scatter(0)
    merge_cores(2)
    scatter(1)
    scatter(2)
    stage3(2)
    for stage, (took, gave) in enumerate(((x1, x2), (x2, x3))):
        for part in range(3):
            axis = ORDERS[part][stage + 1]
            wait(took[part].at[0:3], xr.at[stage, part])
            gave[part][pos[axis]] = (took[part][0] + took[part][1]) + (took[part][2] + took[part][3])
            here = gave[part].at[pos[axis]]
            for step in (2, 1, 3):
                remote(here, here, xs.at[stage + 1, part], xr.at[stage + 1, part], beside(axis, step))
            sent.append((gave[part].at[0:3], xs.at[stage + 1, part]))
        if stage == 0:
            stage3(1, 3)
    early = list(sent)
    sent.clear()
    for part in range(3):
        axis, size = ORDERS[part][0], QUARTER[part]
        wait(x3[part].at[0:3], xr.at[2, part])
        rows = pl.ds(pl.multiple_of(QFIRST[part] + pos[axis] * size, 8), size)
        gw_out[rows, kept] = (x3[part][0] + x3[part][1]) + (x3[part][2] + x3[part][3])
        here = gw_out.at[rows, kept]
        for step in (2, 1, 3):
            remote(here, here, xs.at[3, part], xr.at[3, part], beside(axis, step))
        remote(here, here, fs.at[0, part], fr.at[0, part], partner)
        sent.append((x3[part].at[0:3], xs.at[3, part]))
        sent.append((x3[part].at[0], fs.at[0, part]))

    for part in range(3):
        for b in range(3):
            wait(rd[part].at[b], r3.at[part, b])
        rows = slice(FIRST[part], FIRST[part] + ROWS[part])
        tot[rows] = (full[part][0, 0, 0] + rd[part][0]) + (rd[part][1] + rd[part][2])
    high, low = split(tot[...].T)
    get_w.wait()
    last = (((1,), (1,)), ((), ()))
    gf[...] = lax.dot_general(high, w_ref[...], last, preferred_element_type=F32) + lax.dot_general(
        low, w_ref[...], last, preferred_element_type=F32
    )

    for region, sem in early:
        wait(region, sem)

    for part in range(3):
        axis, size = ORDERS[part][0], QUARTER[part]
        wait(x3[part].at[0:3], xr.at[3, part])
        for step in (1, 2, 3):
            rows = pl.ds(pl.multiple_of(QFIRST[part] + ((pos[axis] + step) % 4) * size, 8), size)
            here = gw_out.at[rows, kept]
            remote(here, here, fs.at[1, part], fr.at[1, part], partner)
        sent.append((x3[part].at[0:3], fs.at[1, part]))
    for part in range(3):
        wait(x3[part].at[0], fr.at[0, part])
        wait(x3[part].at[0:3], fr.at[1, part])
    finish()


def body(tile_values, tile_rows, tile_cols, tile_counts, grad_out, features, weight):
    tiles = tile_values[0, 0, :, 0]
    anywhere = pl.BlockSpec(memory_space=pl.ANY)
    smem = pl.BlockSpec(memory_space=pltpu.SMEM)

    def per_part(*shape, dtype, rows=ROWS, lanes=128):
        return [pltpu.VMEM((*shape, r, lanes), dtype) for r in rows]

    dma = pltpu.SemaphoreType.DMA
    scratch = [
        pltpu.VMEM((32, 256, 128), BF16),
        pltpu.VMEM((32, 256, 128), BF16),
        pltpu.VMEM((32, 128), F32),
        pltpu.VMEM((32, 128), F32),
        pltpu.VMEM((512, 512), BF16),
        pltpu.VMEM((512, 512), BF16),
        pltpu.VMEM((512, 512), BF16),
        pltpu.VMEM((3, 4, 128, 512), BF16),
        *per_part(4, 4, 4, dtype=BF16),
        *per_part(4, 4, 4, dtype=F32),
        *per_part(2, 4, 2, dtype=BF16),
        *per_part(2, 4, 4, dtype=BF16),
        *per_part(2, 2, dtype=BF16),
        *per_part(2, 4, dtype=BF16),
        *per_part(3, dtype=F32),
        pltpu.VMEM((512, 128), F32),
        pltpu.VMEM((512, 512), F32),
        pltpu.VMEM((512, 256), F32),
        pltpu.VMEM((512, 256), F32),
    ]
    for _ in range(3):
        scratch += per_part(4, dtype=F32, rows=QUARTER, lanes=256)
    scratch += [
        dma((5,)),
        dma((3,)),
        dma((3,)),
        dma((4,)),
        dma((4,)),
        dma((4,)),
        dma,
        dma,
        dma((3, 4)),
        dma((3, 2, 4)),
        dma((3, 2, 4)),
        dma((2,)),
        dma((3, 4)),
        dma((3, 4)),
        dma((3, 3)),
        dma((3, 3)),
        dma((3,)),
        dma((3,)),
        dma((4, 3)),
        dma((4, 3)),
        dma((2, 3)),
        dma((2, 3)),
    ]
    vmem = pl.BlockSpec(memory_space=pltpu.VMEM)
    grad_features, turned = pl.pallas_call(
        kernel,
        out_shape=(pltpu.VMEM((128, 512), F32), pltpu.VMEM((512, 512), F32)),
        in_specs=[smem, smem, smem, anywhere, anywhere, anywhere, anywhere],
        out_specs=(vmem, vmem),
        scratch_shapes=scratch,
        compiler_params=pltpu.CompilerParams(
            collective_id=0, has_side_effects=True, vmem_limit_bytes=56 * 1024 * 1024
        ),
    )(tile_rows[..., 0], tile_cols[..., 0], tile_counts, tiles, grad_out, features, weight)
    return grad_features, turned.T


def solution(mesh):
    placed = (
        P("blk", "rep", None, None, None, None),
        P("blk", "rep", None, None),
        P("blk", "rep", None, None),
        P("blk", "rep", None),
        P("blk", None),
        P(("blk", "rep"), None),
        P(),
    )
    return jax.shard_map(
        body, mesh=mesh, in_specs=placed, out_specs=(P(("blk", "rep"), None), P()), check_vma=False
    )
```

```python
import functools

import jax
import jax.numpy as jnp
from jax import lax
from jax.experimental import pallas as pl
from jax.experimental.pallas import tpu as pltpu
from jax.sharding import PartitionSpec as P

MESH = pl.DeviceIdType.MESH
F32 = jnp.float32
BF16 = jnp.bfloat16

ROWS = (176, 176, 160)
FIRST = (0, 176, 352)
X, Y, Z = 0, 1, 2
ORDERS = ((X, Z, Y), (Y, X, Z), (Z, Y, X))
QUARTER = (24, 24, 16, 24, 24, 16)
QFIRST = (0, 96, 192, 256, 352, 448)
PLACES = (2, 1, 3, 0)


def kernel(rows_ref, cols_ref, counts_ref, tiles_ref, g_any, x_any, w_any, gf, gw_out, *scratch):
    (t0, t1, code0, code1, g_ref, w_ref, gt, xg, *rest) = scratch
    send = rest[0:3]
    full = rest[3:6]
    ra, rb, r2a, rc, rd = rest[6:9], rest[9:12], rest[12:15], rest[15:18], rest[18:21]
    tot, gw, gwr, half = rest[21:25]
    x1, x2, x3 = rest[25:31], rest[31:37], rest[37:43]
    (ins, gs, gr, tl, ts, tr, cs, cr, s1, ras, rbs, rps, s2, r2, s3, r3, es, er, xs, xr, fs, fr) = rest[43:]

    blk = lax.axis_index("blk")
    rep = lax.axis_index("rep")
    core = rep % 2
    pos = (blk // 8, (blk // 2) % 4, (rep // 2) * 2 + blk % 2)

    def device(where, which):
        return (where[0] * 8 + where[1] * 2 + where[2] % 2, (where[2] // 2) * 2 + which)

    def beside(axis, step):
        where = list(pos)
        where[axis] = (pos[axis] + step) % 4
        return device(where, core)

    partner = device(pos, 1 - core)

    def remote(src, dst, ssem, rsem, to):
        pltpu.make_async_remote_copy(
            src_ref=src, dst_ref=dst, send_sem=ssem, recv_sem=rsem, device_id=to, device_id_type=MESH
        ).start()

    def wait(ref, sem):
        pltpu.make_async_copy(ref, ref, sem).wait()

    mine = pl.ds(pl.multiple_of(core * 128, 128), 128)
    other = pl.ds(pl.multiple_of((1 - core) * 128, 128), 128)

    barrier = pltpu.get_barrier_semaphore()
    for axis in (X, Y, Z):
        for step in (2, 1, 3):
            pl.semaphore_signal(barrier, inc=1, device_id=beside(axis, step), device_id_type=MESH)
    pl.semaphore_signal(barrier, inc=1, device_id=partner, device_id_type=MESH)

    def columns(n):
        return pl.ds(((pos[0] + PLACES[n]) % 4) * 8, 8)

    def fetch(src, dst, sem):
        copy = pltpu.make_async_copy(src, dst, sem)
        copy.start()
        return copy

    get_g = fetch(g_any, g_ref, ins.at[0])
    for n in range(4):
        fetch(tiles_ref.at[columns(n), :, mine], t0.at[8 * n : 8 * n + 8], tl.at[n])
    get_x = [fetch(x_any, xg.at[axis, 3], ins.at[1 + axis]) for axis in (X, Y, Z)]
    get_w = fetch(w_any, w_ref, ins.at[4])

    sent = []

    def finish():
        for region, sem in sent:
            wait(region, sem)

    for c in range(32):
        spot = rows_ref[0, 0, c] * 2 + cols_ref[0, 0, c]
        used = jnp.where(counts_ref[0, 0, c] > 0, spot, -1)
        code0[c : c + 1, :] = jnp.full((1, 128), used, jnp.int32).astype(F32)
    pl.semaphore_wait(barrier, 10)

    def swap(n):
        slots = slice(8 * n, 8 * n + 8)
        remote(tiles_ref.at[columns(n), :, other], t1.at[slots], ts.at[n], tr.at[n], partner)
        sent.append((t1.at[slots], ts.at[n]))

    remote(code0, code1, cs, cr, partner)
    sent.append((code0, cs))
    swap(0)
    for axis in (X, Y, Z):
        for step in (2, 1, 3):
            remote(x_any, xg.at[axis, step - 1], gs.at[axis], gr.at[axis], beside(axis, step))
        sent.append((xg.at[axis, 0:3], gs.at[axis]))
    for n in range(1, 4):
        swap(n)
    get_g.wait()
    gt[...] = g_ref[...].T
    for get in get_x:
        get.wait()
    wait(code1, cr)

    def send_x(dx, dy):
        if dx == 2:
            way = dy // 2
            to = beside(X, 1 + 2 * way)
            remote(send[0].at[2, :, dy], ra[0].at[way, :, dy % 2], s1.at[0, 2], ras.at[0, way, 0], to)
        if dx % 2 == 1:
            way = dx // 2

            @pl.when(dy // 2 != way)
            def _():
                block = send[0].at[dx, :, dy]
                remote(block, rb[0].at[way, :, dy], s1.at[0, dx], rps.at[way], beside(X, dx))

    def send_y(dx, dy):
        @pl.when(dy == 2)
        def _():
            for way in range(2):
                pair = slice(2 * way, 2 * way + 2)
                to = beside(Y, 1 + 2 * way)
                remote(send[1].at[2, dx, pair], ra[1].at[way, dx], s1.at[1, 2], ras.at[1, way, dx], to)

        @pl.when(dy % 2 == 1)
        def _():
            way = dy // 2
            pair = pl.ds(2 - 2 * way, 2)
            block = send[1].at[dy, dx, pair]
            remote(block, rb[1].at[way, dx, pair], s1.at[1, dy], rbs.at[1, way, dx], beside(Y, 1 + 2 * way))

    def send_z(dx, dy):
        way = dx // 2
        to = beside(Z, 1 + 2 * way)
        remote(send[2].at[2, dy, dx], ra[2].at[way, dy, dx % 2], s1.at[2, 2], ras.at[2, way, dy], to)
        way = 1 - way
        at1 = 1 + 2 * way
        remote(send[2].at[at1, dy, dx], rb[2].at[way, dy, dx], s1.at[2, at1], rbs.at[2, way, dy], beside(Z, at1))

    def products(n):
        dx = PLACES[n]
        wait(t0.at[8 * n : 8 * n + 8], tl.at[n])
        wait(t1.at[8 * n : 8 * n + 8], tr.at[n])

        def one(i, carry):
            dy = (i + 2) % 4
            for dl in range(2):
                offset = ((pos[1] + dy) % 4) * 2 + (pos[2] + dl) % 2
                c = ((pos[0] + dx) % 4) * 8 + offset
                near = ((pos[2] + dl) % 4) // 2
                own, theirs = t0[8 * n + offset], t1[8 * n + offset]
                code_own = code0[pl.ds(c, 1), :]
                code_theirs = code1[pl.ds(c, 1), :]
                lines = []
                for row in range(2):
                    line = []
                    for col in (near, 1 - near):
                        key = (row * 2 + col).astype(F32)
                        keep_own = jnp.where(code_own == key, 1.0, 0.0).astype(BF16)
                        keep_theirs = jnp.where(code_theirs == key, 1.0, 0.0).astype(BF16)
                        line.append(own * keep_own + theirs * keep_theirs)
                    lines.append(jnp.concatenate(line, axis=1))
                dense = jnp.concatenate(lines, axis=0)
                made = jnp.dot(gt[...], dense, preferred_element_type=F32)
                for part in range(3):
                    rows = slice(FIRST[part], FIRST[part] + ROWS[part])
                    for side in range(2):
                        block = made[rows, side * 128 : (side + 1) * 128]
                        rel = (dx, dy, dl + 2 * side)
                        at = tuple(rel[axis] for axis in ORDERS[part])
                        fixed = at[0] if isinstance(at[0], int) else 1
                        if fixed != 2:
                            full[part][at] = block
                        if fixed != 0:
                            send[part][at] = block.astype(BF16)
            send_x(dx, dy)
            send_y(dx, dy)
            send_z(dx, dy)
            return carry

        lax.fori_loop(0, 4, one, 0)

    def merge1(part, t):
        axis = ORDERS[part][0]
        for way, at1, low in ((0, 1, 0), (1, 3, 2)):
            if part > 0:
                wait(ra[part].at[way, t], ras.at[part, way, t])
            elif t == 2:
                wait(ra[part].at[way], ras.at[part, way, 0])
            for b in range(2):
                send[part][at1, t, low + b] = (full[part][at1, t, low + b] + ra[part][way, t, b].astype(F32)).astype(BF16)
            pair = slice(low, low + 2)
            remote(
                send[part].at[at1, t, pair],
                rb[part].at[way, t, pair],
                s1.at[part, at1],
                rbs.at[part, way, t],
                beside(axis, 1 + 2 * way),
            )

    def sum1(part, t):
        for way in range(2):
            if part > 0:
                wait(rb[part].at[way, t], rbs.at[part, way, t])
            else:
                wait(rb[part].at[way, t, 0:2], rbs.at[part, way, t])
                if t == 2:
                    wait(rb[part].at[way, :, 0:2], rps.at[way])

        def add(b, carry):
            total = full[part][0, t, b] + rb[part][0, t, b].astype(F32) + rb[part][1, t, b].astype(F32)
            full[part][0, t, b] = total
            send[part][0, t, b] = total.astype(BF16)
            return carry

        lax.fori_loop(0, 4, add, 0)

    def step2(part, t):
        axis = ORDERS[part][1]
        sum1(part, t)
        if t > 0:
            source = send[part].at[0, t]
        if t == 2:
            for way in range(2):
                pair = source.at[2 * way : 2 * way + 2]
                remote(pair, r2a[part].at[way], s2.at[part, 0], r2.at[part, way], beside(axis, 1 + 2 * way))
        elif t > 0:
            way = t // 2
            pair = slice(2 - 2 * way, 4 - 2 * way)
            remote(source.at[pair], rc[part].at[way, pair], s2.at[part, t], r2.at[part, 2 + way], beside(axis, t))

    def merge2(part):
        axis = ORDERS[part][1]
        for way, t in ((0, 1), (1, 3)):
            wait(r2a[part].at[way], r2.at[part, way])
            for b in range(2):
                at = (0, t, 2 * way + b)
                send[part][at] = (full[part][at] + r2a[part][way, b].astype(F32)).astype(BF16)
            pair = slice(2 * way, 2 * way + 2)
            source = send[part].at[0, t, pair]
            remote(source, rc[part].at[way, pair], s2.at[part, t], r2.at[part, 2 + way], beside(axis, t))

    products(0)
    products(1)
    merge1(1, 2)
    products(2)
    products(3)
    for part, t in ((1, 1), (0, 2), (2, 2), (0, 1), (1, 3), (2, 1), (0, 3), (2, 3)):
        merge1(part, t)
    for part in (1, 0, 2):
        step2(part, 2)
        merge1(part, 0)
    for t in (1, 3):
        for part in (1, 0, 2):
            step2(part, t)
            if t == 3:
                merge2(part)
    for part in (1, 0, 2):
        step2(part, 0)
    for part in range(3):
        for at1 in (1, 2, 3):
            sent.append((send[part].at[at1], s1.at[part, at1]))
        for t, sem in ((1, 1), (2, 0), (3, 3)):
            sent.append((send[part].at[0, t], s2.at[part, sem]))

    def stage3(part, *places):
        axis = ORDERS[part][2]
        for b in places:
            remote(full[part].at[0, 0, b], rd[part].at[b - 1], s3.at[part, b - 1], r3.at[part, b - 1], beside(axis, b))
            sent.append((rd[part].at[b - 1], s3.at[part, b - 1]))

    def split(value):
        high = value.astype(BF16)
        return high, (value - high.astype(F32)).astype(BF16)

    kept = pl.ds(pl.multiple_of(core * 256, 256), 256)
    given = pl.ds(pl.multiple_of((1 - core) * 256, 256), 256)
    for part in range(3):
        axis = ORDERS[part][2]
        for way in range(2):
            wait(rc[part].at[way], r2.at[part, 2 + way])
        for b in range(4):
            near, back = (rc[part][way, b].astype(F32) for way in range(2))
            full[part][0, 0, b] = full[part][0, 0, b] + (near + back)
        stage3(part, 2)
        wait(xg.at[axis, 0:3], gr.at[axis])
        high, low = split(jnp.concatenate([full[part][0, 0, b] for b in (3, 2, 1, 0)], axis=1))
        owners = xg[axis].reshape(512, 512)
        rows = slice(FIRST[part], FIRST[part] + ROWS[part])
        gw[rows] = jnp.dot(high, owners, preferred_element_type=F32) + jnp.dot(low, owners, preferred_element_type=F32)
        remote(gw.at[rows, given], gwr.at[rows], es.at[part], er.at[part], partner)
        sent.append((gwr.at[rows], es.at[part]))

    def merge_cores(part):
        rows = slice(FIRST[part], FIRST[part] + ROWS[part])
        wait(gwr.at[rows], er.at[part])
        half[rows] = gw[rows, kept] + gwr[rows]

    def scatter(piece):
        axis, size = ORDERS[piece % 3][0], QUARTER[piece]
        for step in (2, 1, 3):
            quarter = pl.ds(pl.multiple_of(QFIRST[piece] + ((pos[axis] + step) % 4) * size, 8), size)
            remote(half.at[quarter], x1[piece].at[pos[axis]], xs.at[0, piece], xr.at[0, piece], beside(axis, step))
        x1[piece][pos[axis]] = half[pl.ds(pl.multiple_of(QFIRST[piece] + pos[axis] * size, 8), size), :]
        sent.append((x1[piece].at[0:3], xs.at[0, piece]))

    merge_cores(0)
    scatter(0)
    merge_cores(1)
    scatter(1)
    scatter(2)
    merge_cores(2)
    for piece in range(3, 6):
        scatter(piece)
    for part in range(3):
        stage3(part, 1, 3)
    for stage, (took, gave) in enumerate(((x1, x2), (x2, x3))):
        for piece in range(6):
            axis = ORDERS[piece % 3][stage + 1]
            wait(took[piece].at[0:3], xr.at[stage, piece])
            gave[piece][pos[axis]] = (took[piece][0] + took[piece][1]) + (took[piece][2] + took[piece][3])
            here = gave[piece].at[pos[axis]]
            for step in (2, 1, 3):
                remote(here, here, xs.at[stage + 1, piece], xr.at[stage + 1, piece], beside(axis, step))
            sent.append((gave[piece].at[0:3], xs.at[stage + 1, piece]))
    early = list(sent)
    sent.clear()
    for piece in range(6):
        axis, size = ORDERS[piece % 3][0], QUARTER[piece]
        wait(x3[piece].at[0:3], xr.at[2, piece])
        rows = pl.ds(pl.multiple_of(QFIRST[piece] + pos[axis] * size, 8), size)
        gw_out[rows, kept] = (x3[piece][0] + x3[piece][1]) + (x3[piece][2] + x3[piece][3])
        here = gw_out.at[rows, kept]
        for step in (2, 1, 3):
            remote(here, here, xs.at[3, piece], xr.at[3, piece], beside(axis, step))
        remote(here, here, fs.at[0, piece], fr.at[0, piece], partner)
        sent.append((x3[piece].at[0:3], xs.at[3, piece]))
        sent.append((x3[piece].at[0], fs.at[0, piece]))

    for part in range(3):
        for b in range(3):
            wait(rd[part].at[b], r3.at[part, b])
        rows = slice(FIRST[part], FIRST[part] + ROWS[part])
        tot[rows] = (full[part][0, 0, 0] + rd[part][0]) + (rd[part][1] + rd[part][2])
    high, low = split(tot[...].T)
    get_w.wait()
    last = (((1,), (1,)), ((), ()))
    gf[...] = lax.dot_general(high, w_ref[...], last, preferred_element_type=F32) + lax.dot_general(
        low, w_ref[...], last, preferred_element_type=F32
    )

    for region, sem in early:
        wait(region, sem)

    for piece in range(6):
        axis, size = ORDERS[piece % 3][0], QUARTER[piece]
        wait(x3[piece].at[0:3], xr.at[3, piece])
        for step in (1, 2, 3):
            rows = pl.ds(pl.multiple_of(QFIRST[piece] + ((pos[axis] + step) % 4) * size, 8), size)
            here = gw_out.at[rows, kept]
            remote(here, here, fs.at[1, piece], fr.at[1, piece], partner)
        sent.append((x3[piece].at[0:3], fs.at[1, piece]))
    for piece in range(6):
        wait(x3[piece].at[0], fr.at[0, piece])
        wait(x3[piece].at[0:3], fr.at[1, piece])
    finish()


def body(tile_values, tile_rows, tile_cols, tile_counts, grad_out, features, weight):
    tiles = tile_values[0, 0, :, 0]
    anywhere = pl.BlockSpec(memory_space=pl.ANY)
    smem = pl.BlockSpec(memory_space=pltpu.SMEM)

    def per_part(*shape, dtype, rows=ROWS, lanes=128):
        return [pltpu.VMEM((*shape, r, lanes), dtype) for r in rows]

    dma = pltpu.SemaphoreType.DMA
    scratch = [
        pltpu.VMEM((32, 256, 128), BF16),
        pltpu.VMEM((32, 256, 128), BF16),
        pltpu.VMEM((32, 128), F32),
        pltpu.VMEM((32, 128), F32),
        pltpu.VMEM((512, 512), BF16),
        pltpu.VMEM((512, 512), BF16),
        pltpu.VMEM((512, 512), BF16),
        pltpu.VMEM((3, 4, 128, 512), BF16),
        *per_part(4, 4, 4, dtype=BF16),
        *per_part(4, 4, 4, dtype=F32),
        *per_part(2, 4, 2, dtype=BF16),
        *per_part(2, 4, 4, dtype=BF16),
        *per_part(2, 2, dtype=BF16),
        *per_part(2, 4, dtype=BF16),
        *per_part(3, dtype=F32),
        pltpu.VMEM((512, 128), F32),
        pltpu.VMEM((512, 512), F32),
        pltpu.VMEM((512, 256), F32),
        pltpu.VMEM((512, 256), F32),
    ]
    for _ in range(3):
        scratch += per_part(4, dtype=F32, rows=QUARTER, lanes=256)
    scratch += [
        dma((5,)),
        dma((3,)),
        dma((3,)),
        dma((4,)),
        dma((4,)),
        dma((4,)),
        dma,
        dma,
        dma((3, 4)),
        dma((3, 2, 4)),
        dma((3, 2, 4)),
        dma((2,)),
        dma((3, 4)),
        dma((3, 4)),
        dma((3, 3)),
        dma((3, 3)),
        dma((3,)),
        dma((3,)),
        dma((4, 6)),
        dma((4, 6)),
        dma((2, 6)),
        dma((2, 6)),
    ]
    vmem = pl.BlockSpec(memory_space=pltpu.VMEM)
    grad_features, turned = pl.pallas_call(
        kernel,
        out_shape=(pltpu.VMEM((128, 512), F32), pltpu.VMEM((512, 512), F32)),
        in_specs=[smem, smem, smem, anywhere, anywhere, anywhere, anywhere],
        out_specs=(vmem, vmem),
        scratch_shapes=scratch,
        compiler_params=pltpu.CompilerParams(
            collective_id=0, has_side_effects=True, vmem_limit_bytes=56 * 1024 * 1024
        ),
    )(tile_rows[..., 0], tile_cols[..., 0], tile_counts, tiles, grad_out, features, weight)
    return grad_features, turned.T


def solution(mesh):
    placed = (
        P("blk", "rep", None, None, None, None),
        P("blk", "rep", None, None),
        P("blk", "rep", None, None),
        P("blk", "rep", None),
        P("blk", None),
        P(("blk", "rep"), None),
        P(),
    )
    return jax.shard_map(
        body, mesh=mesh, in_specs=placed, out_specs=(P(("blk", "rep"), None), P()), check_vma=False
    )
```

```python
import functools

import jax
import jax.numpy as jnp
from jax import lax
from jax.experimental import pallas as pl
from jax.experimental.pallas import tpu as pltpu
from jax.sharding import PartitionSpec as P

MESH = pl.DeviceIdType.MESH
F32 = jnp.float32
BF16 = jnp.bfloat16

ROWS = (176, 176, 160)
FIRST = (0, 176, 352)
X, Y, Z = 0, 1, 2
ORDERS = ((X, Z, Y), (Y, X, Z), (Z, Y, X))
QUARTER = (16, 16, 16, 16, 16, 16, 16, 8, 8)
QFIRST = (0, 64, 128, 192, 256, 320, 384, 448, 480)
PLACES = (2, 1, 3, 0)


def kernel(rows_ref, cols_ref, counts_ref, tiles_ref, g_any, x_any, w_any, gf, gw_out, *scratch):
    (t0, t1, code0, code1, g_ref, w_ref, gt, xg, *rest) = scratch
    send = rest[0:3]
    full = rest[3:6]
    ra, rb, r2a, rc, rd = rest[6:9], rest[9:12], rest[12:15], rest[15:18], rest[18:21]
    tot, gw, gwr, half = rest[21:25]
    x1, x2, x3 = rest[25:34], rest[34:43], rest[43:52]
    (ins, gs, gr, tl, ts, tr, cs, cr, s1, ras, rbs, rps, s2, r2, s3, r3, es, er, xs, xr, fs, fr) = rest[52:]

    blk = lax.axis_index("blk")
    rep = lax.axis_index("rep")
    core = rep % 2
    pos = (blk // 8, (blk // 2) % 4, (rep // 2) * 2 + blk % 2)

    def device(where, which):
        return (where[0] * 8 + where[1] * 2 + where[2] % 2, (where[2] // 2) * 2 + which)

    def beside(axis, step):
        where = list(pos)
        where[axis] = (pos[axis] + step) % 4
        return device(where, core)

    partner = device(pos, 1 - core)

    def remote(src, dst, ssem, rsem, to):
        pltpu.make_async_remote_copy(
            src_ref=src, dst_ref=dst, send_sem=ssem, recv_sem=rsem, device_id=to, device_id_type=MESH
        ).start()

    def wait(ref, sem):
        pltpu.make_async_copy(ref, ref, sem).wait()

    mine = pl.ds(pl.multiple_of(core * 128, 128), 128)
    other = pl.ds(pl.multiple_of((1 - core) * 128, 128), 128)

    barrier = pltpu.get_barrier_semaphore()
    for axis in (X, Y, Z):
        for step in (2, 1, 3):
            pl.semaphore_signal(barrier, inc=1, device_id=beside(axis, step), device_id_type=MESH)
    pl.semaphore_signal(barrier, inc=1, device_id=partner, device_id_type=MESH)

    def columns(n):
        return pl.ds(((pos[0] + PLACES[n]) % 4) * 8, 8)

    def fetch(src, dst, sem):
        copy = pltpu.make_async_copy(src, dst, sem)
        copy.start()
        return copy

    get_g = fetch(g_any, g_ref, ins.at[0])
    for n in range(4):
        fetch(tiles_ref.at[columns(n), :, mine], t0.at[8 * n : 8 * n + 8], tl.at[n])
    get_x = [fetch(x_any, xg.at[axis, 3], ins.at[1 + axis]) for axis in (X, Y, Z)]
    get_w = fetch(w_any, w_ref, ins.at[4])

    sent = []

    def finish():
        for region, sem in sent:
            wait(region, sem)

    for c in range(32):
        spot = rows_ref[0, 0, c] * 2 + cols_ref[0, 0, c]
        used = jnp.where(counts_ref[0, 0, c] > 0, spot, -1)
        code0[c : c + 1, :] = jnp.full((1, 128), used, jnp.int32).astype(F32)
    pl.semaphore_wait(barrier, 10)

    def swap(n):
        slots = slice(8 * n, 8 * n + 8)
        remote(tiles_ref.at[columns(n), :, other], t1.at[slots], ts.at[n], tr.at[n], partner)
        sent.append((t1.at[slots], ts.at[n]))

    remote(code0, code1, cs, cr, partner)
    sent.append((code0, cs))
    swap(0)
    for axis in (X, Y, Z):
        for step in (2, 1, 3):
            remote(x_any, xg.at[axis, step - 1], gs.at[axis], gr.at[axis], beside(axis, step))
        sent.append((xg.at[axis, 0:3], gs.at[axis]))
    for n in range(1, 4):
        swap(n)
    get_g.wait()
    gt[...] = g_ref[...].T
    for get in get_x:
        get.wait()
    wait(code1, cr)

    def send_x(dx, dy):
        if dx == 2:
            way = dy // 2
            to = beside(X, 1 + 2 * way)
            remote(send[0].at[2, :, dy], ra[0].at[way, :, dy % 2], s1.at[0, 2], ras.at[0, way, 0], to)
        if dx % 2 == 1:
            way = dx // 2

            @pl.when(dy // 2 != way)
            def _():
                block = send[0].at[dx, :, dy]
                remote(block, rb[0].at[way, :, dy], s1.at[0, dx], rps.at[way], beside(X, dx))

    def send_y(dx, dy):
        @pl.when(dy == 2)
        def _():
            for way in range(2):
                pair = slice(2 * way, 2 * way + 2)
                to = beside(Y, 1 + 2 * way)
                remote(send[1].at[2, dx, pair], ra[1].at[way, dx], s1.at[1, 2], ras.at[1, way, dx], to)

        @pl.when(dy % 2 == 1)
        def _():
            way = dy // 2
            pair = pl.ds(2 - 2 * way, 2)
            block = send[1].at[dy, dx, pair]
            remote(block, rb[1].at[way, dx, pair], s1.at[1, dy], rbs.at[1, way, dx], beside(Y, 1 + 2 * way))

    def send_z(dx, dy):
        way = dx // 2
        to = beside(Z, 1 + 2 * way)
        remote(send[2].at[2, dy, dx], ra[2].at[way, dy, dx % 2], s1.at[2, 2], ras.at[2, way, dy], to)
        way = 1 - way
        at1 = 1 + 2 * way
        remote(send[2].at[at1, dy, dx], rb[2].at[way, dy, dx], s1.at[2, at1], rbs.at[2, way, dy], beside(Z, at1))

    def products(n):
        dx = PLACES[n]
        wait(t0.at[8 * n : 8 * n + 8], tl.at[n])
        wait(t1.at[8 * n : 8 * n + 8], tr.at[n])

        def one(i, carry):
            dy = (i + 2) % 4
            for dl in range(2):
                offset = ((pos[1] + dy) % 4) * 2 + (pos[2] + dl) % 2
                c = ((pos[0] + dx) % 4) * 8 + offset
                near = ((pos[2] + dl) % 4) // 2
                own, theirs = t0[8 * n + offset], t1[8 * n + offset]
                code_own = code0[pl.ds(c, 1), :]
                code_theirs = code1[pl.ds(c, 1), :]
                lines = []
                for row in range(2):
                    line = []
                    for col in (near, 1 - near):
                        key = (row * 2 + col).astype(F32)
                        keep_own = jnp.where(code_own == key, 1.0, 0.0).astype(BF16)
                        keep_theirs = jnp.where(code_theirs == key, 1.0, 0.0).astype(BF16)
                        line.append(own * keep_own + theirs * keep_theirs)
                    lines.append(jnp.concatenate(line, axis=1))
                dense = jnp.concatenate(lines, axis=0)
                made = jnp.dot(gt[...], dense, preferred_element_type=F32)
                for part in range(3):
                    rows = slice(FIRST[part], FIRST[part] + ROWS[part])
                    for side in range(2):
                        block = made[rows, side * 128 : (side + 1) * 128]
                        rel = (dx, dy, dl + 2 * side)
                        at = tuple(rel[axis] for axis in ORDERS[part])
                        fixed = at[0] if isinstance(at[0], int) else 1
                        if fixed != 2:
                            full[part][at] = block
                        if fixed != 0:
                            send[part][at] = block.astype(BF16)
            send_x(dx, dy)
            send_y(dx, dy)
            send_z(dx, dy)
            return carry

        lax.fori_loop(0, 4, one, 0)

    def merge1(part, t):
        axis = ORDERS[part][0]
        for way, at1, low in ((0, 1, 0), (1, 3, 2)):
            if part > 0:
                wait(ra[part].at[way, t], ras.at[part, way, t])
            elif t == 2:
                wait(ra[part].at[way], ras.at[part, way, 0])
            for b in range(2):
                send[part][at1, t, low + b] = (full[part][at1, t, low + b] + ra[part][way, t, b].astype(F32)).astype(BF16)
            pair = slice(low, low + 2)
            remote(
                send[part].at[at1, t, pair],
                rb[part].at[way, t, pair],
                s1.at[part, at1],
                rbs.at[part, way, t],
                beside(axis, 1 + 2 * way),
            )

    def sum1(part, t):
        for way in range(2):
            if part > 0:
                wait(rb[part].at[way, t], rbs.at[part, way, t])
            else:
                wait(rb[part].at[way, t, 0:2], rbs.at[part, way, t])
                if t == 2:
                    wait(rb[part].at[way, :, 0:2], rps.at[way])

        def add(b, carry):
            total = full[part][0, t, b] + rb[part][0, t, b].astype(F32) + rb[part][1, t, b].astype(F32)
            full[part][0, t, b] = total
            send[part][0, t, b] = total.astype(BF16)
            return carry

        lax.fori_loop(0, 4, add, 0)

    def step2(part, t):
        axis = ORDERS[part][1]
        sum1(part, t)
        if t > 0:
            source = send[part].at[0, t]
        if t == 2:
            for way in range(2):
                pair = source.at[2 * way : 2 * way + 2]
                remote(pair, r2a[part].at[way], s2.at[part, 0], r2.at[part, way], beside(axis, 1 + 2 * way))
        elif t > 0:
            way = t // 2
            pair = slice(2 - 2 * way, 4 - 2 * way)
            remote(source.at[pair], rc[part].at[way, pair], s2.at[part, t], r2.at[part, 2 + way], beside(axis, t))

    def merge2(part):
        axis = ORDERS[part][1]
        for way, t in ((0, 1), (1, 3)):
            wait(r2a[part].at[way], r2.at[part, way])
            for b in range(2):
                at = (0, t, 2 * way + b)
                send[part][at] = (full[part][at] + r2a[part][way, b].astype(F32)).astype(BF16)
            pair = slice(2 * way, 2 * way + 2)
            source = send[part].at[0, t, pair]
            remote(source, rc[part].at[way, pair], s2.at[part, t], r2.at[part, 2 + way], beside(axis, t))

    products(0)
    products(1)
    merge1(1, 2)
    products(2)
    products(3)
    for part, t in ((1, 1), (0, 2), (1, 3), (0, 1), (2, 2), (0, 3), (2, 1), (2, 3)):
        merge1(part, t)
    for part in (1, 0, 2):
        step2(part, 2)
        merge1(part, 0)
    for t in (1, 3):
        for part in (1, 0, 2):
            step2(part, t)
            if t == 3:
                merge2(part)
    for part in (1, 0, 2):
        step2(part, 0)
    for part in range(3):
        for at1 in (1, 2, 3):
            sent.append((send[part].at[at1], s1.at[part, at1]))
        for t, sem in ((1, 1), (2, 0), (3, 3)):
            sent.append((send[part].at[0, t], s2.at[part, sem]))

    def stage3(part, *places):
        axis = ORDERS[part][2]
        for b in places:
            remote(full[part].at[0, 0, b], rd[part].at[b - 1], s3.at[part, b - 1], r3.at[part, b - 1], beside(axis, b))
            sent.append((rd[part].at[b - 1], s3.at[part, b - 1]))

    def split(value):
        high = value.astype(BF16)
        return high, (value - high.astype(F32)).astype(BF16)

    kept = pl.ds(pl.multiple_of(core * 256, 256), 256)
    given = pl.ds(pl.multiple_of((1 - core) * 256, 256), 256)
    for part in (1, 0, 2):
        axis = ORDERS[part][2]
        for way in range(2):
            wait(rc[part].at[way], r2.at[part, 2 + way])
        for b in range(4):
            near, back = (rc[part][way, b].astype(F32) for way in range(2))
            full[part][0, 0, b] = full[part][0, 0, b] + (near + back)
        stage3(part, 2)
        wait(xg.at[axis, 0:3], gr.at[axis])
        high, low = split(jnp.concatenate([full[part][0, 0, b] for b in (3, 2, 1, 0)], axis=1))
        owners = xg[axis].reshape(512, 512)
        rows = slice(FIRST[part], FIRST[part] + ROWS[part])
        gw[rows] = jnp.dot(high, owners, preferred_element_type=F32) + jnp.dot(low, owners, preferred_element_type=F32)
        remote(gw.at[rows, given], gwr.at[rows], es.at[part], er.at[part], partner)
        sent.append((gwr.at[rows], es.at[part]))

    def merge_cores(part):
        rows = slice(FIRST[part], FIRST[part] + ROWS[part])
        wait(gwr.at[rows], er.at[part])
        half[rows] = gw[rows, kept] + gwr[rows]

    def scatter(piece):
        axis, size = ORDERS[piece % 3][0], QUARTER[piece]
        for step in (2, 1, 3):
            quarter = pl.ds(pl.multiple_of(QFIRST[piece] + ((pos[axis] + step) % 4) * size, 8), size)
            remote(half.at[quarter], x1[piece].at[pos[axis]], xs.at[0, piece], xr.at[0, piece], beside(axis, step))
        x1[piece][pos[axis]] = half[pl.ds(pl.multiple_of(QFIRST[piece] + pos[axis] * size, 8), size), :]
        sent.append((x1[piece].at[0:3], xs.at[0, piece]))

    merge_cores(0)
    scatter(0)
    scatter(1)
    merge_cores(1)
    scatter(2)
    scatter(3)
    scatter(4)
    merge_cores(2)
    for piece in range(5, 9):
        scatter(piece)
    for part in range(3):
        stage3(part, 1, 3)
    for stage, (took, gave) in enumerate(((x1, x2), (x2, x3))):
        for piece in range(9):
            axis = ORDERS[piece % 3][stage + 1]
            wait(took[piece].at[0:3], xr.at[stage, piece])
            gave[piece][pos[axis]] = (took[piece][0] + took[piece][1]) + (took[piece][2] + took[piece][3])
            here = gave[piece].at[pos[axis]]
            for step in (2, 1, 3):
                remote(here, here, xs.at[stage + 1, piece], xr.at[stage + 1, piece], beside(axis, step))
            sent.append((gave[piece].at[0:3], xs.at[stage + 1, piece]))
    early = list(sent)
    sent.clear()
    for piece in range(9):
        axis, size = ORDERS[piece % 3][0], QUARTER[piece]
        wait(x3[piece].at[0:3], xr.at[2, piece])
        rows = pl.ds(pl.multiple_of(QFIRST[piece] + pos[axis] * size, 8), size)
        gw_out[rows, kept] = (x3[piece][0] + x3[piece][1]) + (x3[piece][2] + x3[piece][3])
        here = gw_out.at[rows, kept]
        for step in (2, 1, 3):
            remote(here, here, xs.at[3, piece], xr.at[3, piece], beside(axis, step))
        remote(here, here, fs.at[0, piece], fr.at[0, piece], partner)
        sent.append((x3[piece].at[0:3], xs.at[3, piece]))
        sent.append((x3[piece].at[0], fs.at[0, piece]))

    for part in range(3):
        for b in range(3):
            wait(rd[part].at[b], r3.at[part, b])
        rows = slice(FIRST[part], FIRST[part] + ROWS[part])
        tot[rows] = (full[part][0, 0, 0] + rd[part][0]) + (rd[part][1] + rd[part][2])
    high, low = split(tot[...].T)
    get_w.wait()
    last = (((1,), (1,)), ((), ()))
    gf[...] = lax.dot_general(high, w_ref[...], last, preferred_element_type=F32) + lax.dot_general(
        low, w_ref[...], last, preferred_element_type=F32
    )

    for region, sem in early:
        wait(region, sem)

    for piece in range(9):
        axis, size = ORDERS[piece % 3][0], QUARTER[piece]
        wait(x3[piece].at[0:3], xr.at[3, piece])
        for step in (1, 2, 3):
            rows = pl.ds(pl.multiple_of(QFIRST[piece] + ((pos[axis] + step) % 4) * size, 8), size)
            here = gw_out.at[rows, kept]
            remote(here, here, fs.at[1, piece], fr.at[1, piece], partner)
        sent.append((x3[piece].at[0:3], fs.at[1, piece]))
    for piece in range(9):
        wait(x3[piece].at[0], fr.at[0, piece])
        wait(x3[piece].at[0:3], fr.at[1, piece])
    finish()


def body(tile_values, tile_rows, tile_cols, tile_counts, grad_out, features, weight):
    tiles = tile_values[0, 0, :, 0]
    anywhere = pl.BlockSpec(memory_space=pl.ANY)
    smem = pl.BlockSpec(memory_space=pltpu.SMEM)

    def per_part(*shape, dtype, rows=ROWS, lanes=128):
        return [pltpu.VMEM((*shape, r, lanes), dtype) for r in rows]

    dma = pltpu.SemaphoreType.DMA
    scratch = [
        pltpu.VMEM((32, 256, 128), BF16),
        pltpu.VMEM((32, 256, 128), BF16),
        pltpu.VMEM((32, 128), F32),
        pltpu.VMEM((32, 128), F32),
        pltpu.VMEM((512, 512), BF16),
        pltpu.VMEM((512, 512), BF16),
        pltpu.VMEM((512, 512), BF16),
        pltpu.VMEM((3, 4, 128, 512), BF16),
        *per_part(4, 4, 4, dtype=BF16),
        *per_part(4, 4, 4, dtype=F32),
        *per_part(2, 4, 2, dtype=BF16),
        *per_part(2, 4, 4, dtype=BF16),
        *per_part(2, 2, dtype=BF16),
        *per_part(2, 4, dtype=BF16),
        *per_part(3, dtype=F32),
        pltpu.VMEM((512, 128), F32),
        pltpu.VMEM((512, 512), F32),
        pltpu.VMEM((512, 256), F32),
        pltpu.VMEM((512, 256), F32),
    ]
    for _ in range(3):
        scratch += per_part(4, dtype=F32, rows=QUARTER, lanes=256)
    scratch += [
        dma((5,)),
        dma((3,)),
        dma((3,)),
        dma((4,)),
        dma((4,)),
        dma((4,)),
        dma,
        dma,
        dma((3, 4)),
        dma((3, 2, 4)),
        dma((3, 2, 4)),
        dma((2,)),
        dma((3, 4)),
        dma((3, 4)),
        dma((3, 3)),
        dma((3, 3)),
        dma((3,)),
        dma((3,)),
        dma((4, 9)),
        dma((4, 9)),
        dma((2, 9)),
        dma((2, 9)),
    ]
    vmem = pl.BlockSpec(memory_space=pltpu.VMEM)
    grad_features, turned = pl.pallas_call(
        kernel,
        out_shape=(pltpu.VMEM((128, 512), F32), pltpu.VMEM((512, 512), F32)),
        in_specs=[smem, smem, smem, anywhere, anywhere, anywhere, anywhere],
        out_specs=(vmem, vmem),
        scratch_shapes=scratch,
        compiler_params=pltpu.CompilerParams(
            collective_id=0, has_side_effects=True, vmem_limit_bytes=56 * 1024 * 1024
        ),
    )(tile_rows[..., 0], tile_cols[..., 0], tile_counts, tiles, grad_out, features, weight)
    return grad_features, turned.T


def solution(mesh):
    placed = (
        P("blk", "rep", None, None, None, None),
        P("blk", "rep", None, None),
        P("blk", "rep", None, None),
        P("blk", "rep", None),
        P("blk", None),
        P(("blk", "rep"), None),
        P(),
    )
    return jax.shard_map(
        body, mesh=mesh, in_specs=placed, out_specs=(P(("blk", "rep"), None), P()), check_vma=False
    )
```

```python
import functools

import jax
import jax.numpy as jnp
from jax import lax
from jax.experimental import pallas as pl
from jax.experimental.pallas import tpu as pltpu
from jax.sharding import PartitionSpec as P

MESH = pl.DeviceIdType.MESH
F32 = jnp.float32
BF16 = jnp.bfloat16

ROWS = (176, 176, 160)
FIRST = (0, 176, 352)
X, Y, Z = 0, 1, 2
ORDERS = ((X, Z, Y), (Y, X, Z), (Z, Y, X))
QUARTER = (16, 16, 16, 16, 16, 16, 16, 8, 8)
QFIRST = (0, 64, 128, 192, 256, 320, 384, 448, 480)
PLACES = (2, 1, 3, 0)


def kernel(rows_ref, cols_ref, counts_ref, tiles_ref, g_any, x_any, w_any, gf, gw_out, *scratch):
    (t0, t1, code0, code1, g_ref, w_ref, gt, xg, *rest) = scratch
    send = rest[0:3]
    full = rest[3:6]
    ra, rb, r2a, rc, rd = rest[6:9], rest[9:12], rest[12:15], rest[15:18], rest[18:21]
    tot, gw, gwr, half = rest[21:25]
    x1, x2, x3 = rest[25:34], rest[34:43], rest[43:52]
    (ins, gs, gr, tl, ts, tr, cs, cr, s1, ras, rbs, rps, s2, r2, s3, r3, es, er, xs, xr, fs, fr) = rest[52:]

    blk = lax.axis_index("blk")
    rep = lax.axis_index("rep")
    core = rep % 2
    pos = (blk // 8, (blk // 2) % 4, (rep // 2) * 2 + blk % 2)

    def device(where, which):
        return (where[0] * 8 + where[1] * 2 + where[2] % 2, (where[2] // 2) * 2 + which)

    def beside(axis, step):
        where = list(pos)
        where[axis] = (pos[axis] + step) % 4
        return device(where, core)

    partner = device(pos, 1 - core)

    def remote(src, dst, ssem, rsem, to):
        pltpu.make_async_remote_copy(
            src_ref=src, dst_ref=dst, send_sem=ssem, recv_sem=rsem, device_id=to, device_id_type=MESH
        ).start()

    def wait(ref, sem):
        pltpu.make_async_copy(ref, ref, sem).wait()

    mine = pl.ds(pl.multiple_of(core * 128, 128), 128)
    other = pl.ds(pl.multiple_of((1 - core) * 128, 128), 128)

    barrier = pltpu.get_barrier_semaphore()
    for axis in (X, Y, Z):
        for step in (2, 1, 3):
            pl.semaphore_signal(barrier, inc=1, device_id=beside(axis, step), device_id_type=MESH)
    pl.semaphore_signal(barrier, inc=1, device_id=partner, device_id_type=MESH)

    def columns(n):
        return pl.ds(((pos[0] + PLACES[n]) % 4) * 8, 8)

    def fetch(src, dst, sem):
        copy = pltpu.make_async_copy(src, dst, sem)
        copy.start()
        return copy

    get_g = fetch(g_any, g_ref, ins.at[0])
    for n in range(4):
        fetch(tiles_ref.at[columns(n), :, mine], t0.at[8 * n : 8 * n + 8], tl.at[n])
    get_x = [fetch(x_any, xg.at[axis, 3], ins.at[1 + axis]) for axis in (X, Y, Z)]
    get_w = fetch(w_any, w_ref, ins.at[4])

    sent = []

    def finish():
        for region, sem in sent:
            wait(region, sem)

    for c in range(32):
        spot = rows_ref[0, 0, c] * 2 + cols_ref[0, 0, c]
        used = jnp.where(counts_ref[0, 0, c] > 0, spot, -1)
        code0[c : c + 1, :] = jnp.full((1, 128), used, jnp.int32).astype(F32)
    pl.semaphore_wait(barrier, 10)

    def swap(n):
        slots = slice(8 * n, 8 * n + 8)
        remote(tiles_ref.at[columns(n), :, other], t1.at[slots], ts.at[n], tr.at[n], partner)
        sent.append((t1.at[slots], ts.at[n]))

    remote(code0, code1, cs, cr, partner)
    sent.append((code0, cs))
    swap(0)
    for axis in (X, Y, Z):
        for step in (2, 1, 3):
            remote(x_any, xg.at[axis, step - 1], gs.at[axis], gr.at[axis], beside(axis, step))
        sent.append((xg.at[axis, 0:3], gs.at[axis]))
    for n in range(1, 4):
        swap(n)
    get_g.wait()
    gt[...] = g_ref[...].T
    for get in get_x:
        get.wait()
    wait(code1, cr)

    def send_x(dx, dy):
        if dx == 2:
            way = dy // 2
            to = beside(X, 1 + 2 * way)
            remote(send[0].at[2, :, dy], ra[0].at[way, :, dy % 2], s1.at[0, 2], ras.at[0, way, 0], to)
        if dx % 2 == 1:
            way = dx // 2

            @pl.when(dy // 2 != way)
            def _():
                block = send[0].at[dx, :, dy]
                remote(block, rb[0].at[way, :, dy], s1.at[0, dx], rps.at[way], beside(X, dx))

    def send_y(dx, dy):
        @pl.when(dy == 2)
        def _():
            for way in range(2):
                pair = slice(2 * way, 2 * way + 2)
                to = beside(Y, 1 + 2 * way)
                remote(send[1].at[2, dx, pair], ra[1].at[way, dx], s1.at[1, 2], ras.at[1, way, dx], to)

        @pl.when(dy % 2 == 1)
        def _():
            way = dy // 2
            pair = pl.ds(2 - 2 * way, 2)
            block = send[1].at[dy, dx, pair]
            remote(block, rb[1].at[way, dx, pair], s1.at[1, dy], rbs.at[1, way, dx], beside(Y, 1 + 2 * way))

    def send_z(dx, dy):
        way = dx // 2
        to = beside(Z, 1 + 2 * way)
        remote(send[2].at[2, dy, dx], ra[2].at[way, dy, dx % 2], s1.at[2, 2], ras.at[2, way, dy], to)
        way = 1 - way
        at1 = 1 + 2 * way
        remote(send[2].at[at1, dy, dx], rb[2].at[way, dy, dx], s1.at[2, at1], rbs.at[2, way, dy], beside(Z, at1))

    def products(n):
        dx = PLACES[n]
        wait(t0.at[8 * n : 8 * n + 8], tl.at[n])
        wait(t1.at[8 * n : 8 * n + 8], tr.at[n])

        def one(i, carry):
            dy = (2 + 3 * i) % 4
            for dl in range(2):
                offset = ((pos[1] + dy) % 4) * 2 + (pos[2] + dl) % 2
                c = ((pos[0] + dx) % 4) * 8 + offset
                near = ((pos[2] + dl) % 4) // 2
                own, theirs = t0[8 * n + offset], t1[8 * n + offset]
                code_own = code0[pl.ds(c, 1), :]
                code_theirs = code1[pl.ds(c, 1), :]
                lines = []
                for row in range(2):
                    line = []
                    for col in (near, 1 - near):
                        key = (row * 2 + col).astype(F32)
                        keep_own = jnp.where(code_own == key, 1.0, 0.0).astype(BF16)
                        keep_theirs = jnp.where(code_theirs == key, 1.0, 0.0).astype(BF16)
                        line.append(own * keep_own + theirs * keep_theirs)
                    lines.append(jnp.concatenate(line, axis=1))
                dense = jnp.concatenate(lines, axis=0)
                made = jnp.dot(gt[...], dense, preferred_element_type=F32)
                for part in range(3):
                    rows = slice(FIRST[part], FIRST[part] + ROWS[part])
                    for side in range(2):
                        block = made[rows, side * 128 : (side + 1) * 128]
                        rel = (dx, dy, dl + 2 * side)
                        at = tuple(rel[axis] for axis in ORDERS[part])
                        fixed = at[0] if isinstance(at[0], int) else 1
                        if fixed != 2:
                            full[part][at] = block
                        if fixed != 0:
                            send[part][at] = block.astype(BF16)
            send_x(dx, dy)
            send_y(dx, dy)
            send_z(dx, dy)
            return carry

        lax.fori_loop(0, 4, one, 0)

    def merge1(part, t):
        axis = ORDERS[part][0]
        for way, at1, low in ((0, 1, 0), (1, 3, 2)):
            if part > 0:
                wait(ra[part].at[way, t], ras.at[part, way, t])
            elif t == 2:
                wait(ra[part].at[way], ras.at[part, way, 0])
            for b in range(2):
                send[part][at1, t, low + b] = (full[part][at1, t, low + b] + ra[part][way, t, b].astype(F32)).astype(BF16)
            pair = slice(low, low + 2)
            remote(
                send[part].at[at1, t, pair],
                rb[part].at[way, t, pair],
                s1.at[part, at1],
                rbs.at[part, way, t],
                beside(axis, 1 + 2 * way),
            )

    def sum1(part, t):
        for way in range(2):
            if part > 0:
                wait(rb[part].at[way, t], rbs.at[part, way, t])
            else:
                wait(rb[part].at[way, t, 0:2], rbs.at[part, way, t])
                if t == 2:
                    wait(rb[part].at[way, :, 0:2], rps.at[way])

        def add(b, carry):
            total = full[part][0, t, b] + rb[part][0, t, b].astype(F32) + rb[part][1, t, b].astype(F32)
            full[part][0, t, b] = total
            send[part][0, t, b] = total.astype(BF16)
            return carry

        lax.fori_loop(0, 4, add, 0)

    def step2(part, t):
        axis = ORDERS[part][1]
        sum1(part, t)
        if t > 0:
            source = send[part].at[0, t]
        if t == 2:
            for way in range(2):
                pair = source.at[2 * way : 2 * way + 2]
                remote(pair, r2a[part].at[way], s2.at[part, 0], r2.at[part, way], beside(axis, 1 + 2 * way))
        elif t > 0:
            way = t // 2
            pair = slice(2 - 2 * way, 4 - 2 * way)
            remote(source.at[pair], rc[part].at[way, pair], s2.at[part, t], r2.at[part, 2 + way], beside(axis, t))

    def merge2(part):
        axis = ORDERS[part][1]
        for way, t in ((0, 1), (1, 3)):
            wait(r2a[part].at[way], r2.at[part, way])
            for b in range(2):
                at = (0, t, 2 * way + b)
                send[part][at] = (full[part][at] + r2a[part][way, b].astype(F32)).astype(BF16)
            pair = slice(2 * way, 2 * way + 2)
            source = send[part].at[0, t, pair]
            remote(source, rc[part].at[way, pair], s2.at[part, t], r2.at[part, 2 + way], beside(axis, t))

    products(0)
    products(1)
    merge1(1, 2)
    products(2)
    products(3)
    for part, t in ((1, 1), (0, 2), (1, 3), (0, 1), (2, 2), (0, 3), (2, 1), (2, 3)):
        merge1(part, t)
    for part in (1, 0, 2):
        step2(part, 2)
        merge1(part, 0)
    for t in (1, 3):
        for part in (1, 0, 2):
            step2(part, t)
            if t == 3:
                merge2(part)
    for part in (1, 0, 2):
        step2(part, 0)
    for part in range(3):
        for at1 in (1, 2, 3):
            sent.append((send[part].at[at1], s1.at[part, at1]))
        for t, sem in ((1, 1), (2, 0), (3, 3)):
            sent.append((send[part].at[0, t], s2.at[part, sem]))

    def stage3(part, *places):
        axis = ORDERS[part][2]
        for b in places:
            remote(full[part].at[0, 0, b], rd[part].at[b - 1], s3.at[part, b - 1], r3.at[part, b - 1], beside(axis, b))
            sent.append((rd[part].at[b - 1], s3.at[part, b - 1]))

    def split(value):
        high = value.astype(BF16)
        return high, (value - high.astype(F32)).astype(BF16)

    kept = pl.ds(pl.multiple_of(core * 256, 256), 256)
    given = pl.ds(pl.multiple_of((1 - core) * 256, 256), 256)
    for part in (1, 0, 2):
        axis = ORDERS[part][2]
        for way in range(2):
            wait(rc[part].at[way], r2.at[part, 2 + way])
        for b in range(4):
            near, back = (rc[part][way, b].astype(F32) for way in range(2))
            full[part][0, 0, b] = full[part][0, 0, b] + (near + back)
        stage3(part, 2)
        wait(xg.at[axis, 0:3], gr.at[axis])
        high, low = split(jnp.concatenate([full[part][0, 0, b] for b in (3, 2, 1, 0)], axis=1))
        owners = xg[axis].reshape(512, 512)
        rows = slice(FIRST[part], FIRST[part] + ROWS[part])
        gw[rows] = jnp.dot(high, owners, preferred_element_type=F32) + jnp.dot(low, owners, preferred_element_type=F32)
        remote(gw.at[rows, given], gwr.at[rows], es.at[part], er.at[part], partner)
        sent.append((gwr.at[rows], es.at[part]))

    def merge_cores(part):
        rows = slice(FIRST[part], FIRST[part] + ROWS[part])
        wait(gwr.at[rows], er.at[part])
        half[rows] = gw[rows, kept] + gwr[rows]

    def scatter(piece):
        axis, size = ORDERS[piece % 3][0], QUARTER[piece]
        for step in (2, 1, 3):
            quarter = pl.ds(pl.multiple_of(QFIRST[piece] + ((pos[axis] + step) % 4) * size, 8), size)
            remote(half.at[quarter], x1[piece].at[pos[axis]], xs.at[0, piece], xr.at[0, piece], beside(axis, step))
        x1[piece][pos[axis]] = half[pl.ds(pl.multiple_of(QFIRST[piece] + pos[axis] * size, 8), size), :]
        sent.append((x1[piece].at[0:3], xs.at[0, piece]))

    merge_cores(0)
    scatter(0)
    scatter(1)
    merge_cores(1)
    scatter(2)
    scatter(3)
    scatter(4)
    merge_cores(2)
    for piece in range(5, 9):
        scatter(piece)
    for part in range(3):
        stage3(part, 1)
    for stage, (took, gave) in enumerate(((x1, x2), (x2, x3))):
        for piece in range(9):
            axis = ORDERS[piece % 3][stage + 1]
            wait(took[piece].at[0:3], xr.at[stage, piece])
            gave[piece][pos[axis]] = (took[piece][0] + took[piece][1]) + (took[piece][2] + took[piece][3])
            here = gave[piece].at[pos[axis]]
            for step in (2, 1, 3):
                remote(here, here, xs.at[stage + 1, piece], xr.at[stage + 1, piece], beside(axis, step))
            sent.append((gave[piece].at[0:3], xs.at[stage + 1, piece]))
        if stage == 0:
            for part in range(3):
                stage3(part, 3)
    early = list(sent)
    sent.clear()
    for piece in range(9):
        axis, size = ORDERS[piece % 3][0], QUARTER[piece]
        wait(x3[piece].at[0:3], xr.at[2, piece])
        rows = pl.ds(pl.multiple_of(QFIRST[piece] + pos[axis] * size, 8), size)
        gw_out[rows, kept] = (x3[piece][0] + x3[piece][1]) + (x3[piece][2] + x3[piece][3])
        here = gw_out.at[rows, kept]
        for step in (2, 1, 3):
            remote(here, here, xs.at[3, piece], xr.at[3, piece], beside(axis, step))
        remote(here, here, fs.at[0, piece], fr.at[0, piece], partner)
        sent.append((x3[piece].at[0:3], xs.at[3, piece]))
        sent.append((x3[piece].at[0], fs.at[0, piece]))

    for part in range(3):
        for b in range(3):
            wait(rd[part].at[b], r3.at[part, b])
        rows = slice(FIRST[part], FIRST[part] + ROWS[part])
        tot[rows] = (full[part][0, 0, 0] + rd[part][0]) + (rd[part][1] + rd[part][2])
    high, low = split(tot[...].T)
    get_w.wait()
    last = (((1,), (1,)), ((), ()))
    gf[...] = lax.dot_general(high, w_ref[...], last, preferred_element_type=F32) + lax.dot_general(
        low, w_ref[...], last, preferred_element_type=F32
    )

    for region, sem in early:
        wait(region, sem)

    for piece in range(9):
        axis, size = ORDERS[piece % 3][0], QUARTER[piece]
        wait(x3[piece].at[0:3], xr.at[3, piece])
        for step in (1, 2, 3):
            rows = pl.ds(pl.multiple_of(QFIRST[piece] + ((pos[axis] + step) % 4) * size, 8), size)
            here = gw_out.at[rows, kept]
            remote(here, here, fs.at[1, piece], fr.at[1, piece], partner)
        sent.append((x3[piece].at[0:3], fs.at[1, piece]))
    for piece in range(9):
        wait(x3[piece].at[0], fr.at[0, piece])
        wait(x3[piece].at[0:3], fr.at[1, piece])
    finish()


def body(tile_values, tile_rows, tile_cols, tile_counts, grad_out, features, weight):
    tiles = tile_values[0, 0, :, 0]
    anywhere = pl.BlockSpec(memory_space=pl.ANY)
    smem = pl.BlockSpec(memory_space=pltpu.SMEM)

    def per_part(*shape, dtype, rows=ROWS, lanes=128):
        return [pltpu.VMEM((*shape, r, lanes), dtype) for r in rows]

    dma = pltpu.SemaphoreType.DMA
    scratch = [
        pltpu.VMEM((32, 256, 128), BF16),
        pltpu.VMEM((32, 256, 128), BF16),
        pltpu.VMEM((32, 128), F32),
        pltpu.VMEM((32, 128), F32),
        pltpu.VMEM((512, 512), BF16),
        pltpu.VMEM((512, 512), BF16),
        pltpu.VMEM((512, 512), BF16),
        pltpu.VMEM((3, 4, 128, 512), BF16),
        *per_part(4, 4, 4, dtype=BF16),
        *per_part(4, 4, 4, dtype=F32),
        *per_part(2, 4, 2, dtype=BF16),
        *per_part(2, 4, 4, dtype=BF16),
        *per_part(2, 2, dtype=BF16),
        *per_part(2, 4, dtype=BF16),
        *per_part(3, dtype=F32),
        pltpu.VMEM((512, 128), F32),
        pltpu.VMEM((512, 512), F32),
        pltpu.VMEM((512, 256), F32),
        pltpu.VMEM((512, 256), F32),
    ]
    for _ in range(3):
        scratch += per_part(4, dtype=F32, rows=QUARTER, lanes=256)
    scratch += [
        dma((5,)),
        dma((3,)),
        dma((3,)),
        dma((4,)),
        dma((4,)),
        dma((4,)),
        dma,
        dma,
        dma((3, 4)),
        dma((3, 2, 4)),
        dma((3, 2, 4)),
        dma((2,)),
        dma((3, 4)),
        dma((3, 4)),
        dma((3, 3)),
        dma((3, 3)),
        dma((3,)),
        dma((3,)),
        dma((4, 9)),
        dma((4, 9)),
        dma((2, 9)),
        dma((2, 9)),
    ]
    vmem = pl.BlockSpec(memory_space=pltpu.VMEM)
    grad_features, turned = pl.pallas_call(
        kernel,
        out_shape=(pltpu.VMEM((128, 512), F32), pltpu.VMEM((512, 512), F32)),
        in_specs=[smem, smem, smem, anywhere, anywhere, anywhere, anywhere],
        out_specs=(vmem, vmem),
        scratch_shapes=scratch,
        compiler_params=pltpu.CompilerParams(
            collective_id=0, has_side_effects=True, vmem_limit_bytes=56 * 1024 * 1024
        ),
    )(tile_rows[..., 0], tile_cols[..., 0], tile_counts, tiles, grad_out, features, weight)
    return grad_features, turned.T


def solution(mesh):
    placed = (
        P("blk", "rep", None, None, None, None),
        P("blk", "rep", None, None),
        P("blk", "rep", None, None),
        P("blk", "rep", None),
        P("blk", None),
        P(("blk", "rep"), None),
        P(),
    )
    return jax.shard_map(
        body, mesh=mesh, in_specs=placed, out_specs=(P(("blk", "rep"), None), P()), check_vma=False
    )
```
